256 devices in a mesh: hist: 32 (over z, y), second: 8 (over x, core).
Axes of the slice: x: 4, y: 4, z: 8, core: 2. Of those that a mesh axis runs over, the one named last changes fastest.
Arguments:
- history: bfloat16 [128, 64, 128, 2, 128], P('hist', None, 'second'), may hold values from -0.29882812 to 0.29882812
- row_now: float32 [64, 128, 256], P('hist', 'second'), may hold values from -4.2 to 4.2
- coupling: float32 [64, 64], P('hist'), may hold values from 0.5 to 1.5
- step_inverse: float32 [3, 2, 64, 64], replicated, may hold values from -0.5 to 0.5
- start_step: int32 [1], replicated, may hold values from 64 to 124
- history_time: int32 [128], P('hist'), may hold values from 0 to 127, each once
Outputs:
- green_next: float32 [64, 128, 256], P('hist', 'second')
The draws below stay inside these ranges and needn't reach their ends.
Inputs may be any that keep to these rules, and one draw needn't show every extreme that they name: history_time holds every time from 0 to 127 once.
All inputs are finite; a program needn't handle non-finite values.
Results may differ from the reference program's by a relative error of at most 0.011.
Values may be sent and summed in bfloat16 or wider, within the bound.
A program may use at most 64 MiB of HBM per device.

```python
import math
import jax
import jax.numpy as jnp
from jax import lax

ORBITALS = 64
SLOTS_DEV = 4
STEPS = 3
TIMES = 128
N_HIST = 32


def strengthened(drawn, rng, source, target, parts, factor):
    def block_of(dim):
        return (jnp.arange(drawn.shape[dim]) // (drawn.shape[dim] // parts)).reshape((-1,) + (1,) * (drawn.ndim - 1 - dim))

    first = jax.random.permutation(rng, parts)[block_of(target)]
    second = (block_of(target) + parts // 2) % parts
    return jnp.where((block_of(source) == first) | (block_of(source) == second), factor * drawn, drawn)


def steps_of(key, dims, shards, least, high):
    loudness = 1.0
    for dim, blocks in shards:
        draws = jax.random.uniform(jax.random.fold_in(jax.random.fold_in(key, 6), dim), (blocks,), jnp.float32, least / len(shards), high / len(shards))
        loudness = loudness * jnp.repeat(jnp.exp(draws), dims[dim] // blocks).reshape((-1,) + (1,) * (len(dims) - 1 - dim))
    return loudness


def bell_draw(stream_key, extent, deviation, reach, cuts=(), kind=jnp.bfloat16):
    array = jax.random.normal(stream_key, extent, jnp.float32) * deviation
    if len(cuts) > 0:
        array = steps_of(stream_key, extent, cuts, -0.22, 0.18) * array
    return jnp.clip(array, min=-reach, max=reach).astype(kind)


def bell_draw_with(key, shape, width, limit, shards, heavy, held_as=jnp.bfloat16):
    result = width * jax.random.normal(key, shape, jnp.float32)
    if shards:
        result = result * steps_of(key, shape, shards, -0.22, 0.18)
    return jnp.clip(strengthened(result, jax.random.fold_in(key, 3), *heavy), -limit, limit).astype(held_as)


def setup_inputs(seed: int = 0) -> dict:
    keys = jax.random.split(jax.random.key(seed), 7)
    return {
        "history": bell_draw_with(keys[0], (TIMES, ORBITALS, TIMES, 2, 2 * ORBITALS), 0.05, 0.29882812, ((0, 32), (2, 8)), (0, 4, 32, 2.75)),
        "row_now": bell_draw(keys[1], (ORBITALS, TIMES, 4 * ORBITALS), 0.7, 4.2, ((0, 32), (1, 8)), jnp.float32),
        "coupling": jnp.clip(jnp.exp(math.log(1.5) - 1.0986123 * jax.random.uniform(keys[2], (ORBITALS, ORBITALS), jnp.float32) ** steps_of(keys[2], (ORBITALS, ORBITALS), ((0, 32),), -0.2, 0.2)), 0.5, 1.5),
        "step_inverse": bell_draw(keys[3], (STEPS, 2, ORBITALS, ORBITALS), (2 * ORBITALS) ** -0.5, 0.5, (), jnp.float32),
        "start_step": jax.random.randint(keys[4], (1,), TIMES // 2, TIMES - 3).astype(jnp.int32),
        "history_time": jax.random.permutation(keys[5], TIMES).astype(jnp.int32),
    }


step_width = 0.05
highest = lax.Precision.HIGHEST


def cubic_term(first_real, first_imag, other_real, other_imag):
    square_real = first_real * first_real - first_imag * first_imag
    square_imag = 2.0 * first_real * first_imag
    return (square_real * other_real + square_imag * other_imag,
            square_imag * other_real - square_real * other_imag)


def self_energy(green_row, coupling):
    weight_sq = (coupling * coupling)[:, None, :]
    lesser_real, lesser_imag = green_row[:, :, 0, 0], green_row[:, :, 0, 1]
    greater_real, greater_imag = green_row[:, :, 1, 0], green_row[:, :, 1, 1]
    less_real, less_imag = cubic_term(lesser_real, lesser_imag, greater_real, greater_imag)
    more_real, more_imag = cubic_term(greater_real, greater_imag, lesser_real, lesser_imag)
    diff_real = weight_sq * (more_real - less_real)
    diff_imag = weight_sq * (more_imag - less_imag)
    stacked = jnp.stack([diff_real, diff_imag], axis=2)
    return stacked.reshape(green_row.shape[0], green_row.shape[1], 2 * green_row.shape[4]).astype(jnp.bfloat16)


def advance(green_row, summed, inverse_pair):
    real_sum = summed[:, :, :, 0, 0, :] - summed[:, :, :, 1, 1, :]
    imag_sum = summed[:, :, :, 1, 0, :] + summed[:, :, :, 0, 1, :]
    moved_real = green_row[:, :, :, 0, :] + step_width * real_sum
    moved_imag = green_row[:, :, :, 1, :] + step_width * imag_sum
    inverse_real = inverse_pair[0]
    inverse_imag = inverse_pair[1]
    new_real = (jnp.einsum("xa,btma->btmx", inverse_real, moved_real, precision=highest)
                - jnp.einsum("xa,btma->btmx", inverse_imag, moved_imag, precision=highest))
    new_imag = (jnp.einsum("xa,btma->btmx", inverse_real, moved_imag, precision=highest)
                + jnp.einsum("xa,btma->btmx", inverse_imag, moved_real, precision=highest))
    return jnp.stack([new_real, new_imag], axis=3)


def reference(history, row_now, coupling, step_inverse, start_step, history_time):
    anchor = start_step[0]
    alive_slot = history_time <= anchor
    green_row = row_now.reshape(ORBITALS, TIMES, 2, 2, ORBITALS)
    earlier = []
    for window_step in range(STEPS):
        energy = self_energy(green_row, coupling)
        energy_left = energy.reshape(ORBITALS, TIMES, 2, ORBITALS)
        selected = jnp.take(energy_left, history_time, axis=1)
        selected = jnp.where(alive_slot[None, :, None, None], selected, jnp.zeros((), jnp.bfloat16))

        def add_block(block_index, running):
            first_slot = (block_index * SLOTS_DEV).astype(jnp.int32)
            history_block = lax.dynamic_slice_in_dim(history, first_slot, SLOTS_DEV, 0).astype(jnp.float32)
            history_block = history_block.reshape(SLOTS_DEV, ORBITALS, TIMES, 2, ORBITALS, 2)
            left_rows = lax.dynamic_slice_in_dim(selected, first_slot, SLOTS_DEV, 1).astype(jnp.float32)
            return running + jnp.einsum("jsqa,sjtmbp->btmpqa", left_rows, history_block)

        summed = lax.fori_loop(0, N_HIST, add_block,
                               jnp.zeros((ORBITALS, TIMES, 2, 2, 2, ORBITALS), jnp.float32))
        for past_index, past_row in enumerate(earlier):
            column = lax.dynamic_index_in_dim(energy_left, (anchor + 1 + past_index).astype(jnp.int32), 1,
                                              keepdims=False).astype(jnp.float32)
            summed = summed + jnp.einsum("jqa,btmpj->btmpqa", column, past_row, precision=highest)
        green_row = advance(green_row, summed, step_inverse[window_step])
        earlier.append(green_row)
    return green_row.reshape(ORBITALS, TIMES, 4 * ORBITALS)
```

```python
import functools

import jax
import jax.numpy as jnp
from jax import lax
from jax.experimental import pallas as pl
from jax.experimental.pallas import tpu as pltpu
from jax.sharding import PartitionSpec as P

MESH = pl.DeviceIdType.MESH
HIGHEST = lax.Precision.HIGHEST
STEP_WIDTH = 0.05
CHIPS_Y = 4
F32 = jnp.float32
BF16 = jnp.bfloat16


def cubic_term(first_real, first_imag, other_real, other_imag):
    square_real = first_real * first_real - first_imag * first_imag
    square_imag = 2.0 * first_real * first_imag
    return (
        square_real * other_real + square_imag * other_imag,
        square_imag * other_real - square_real * other_imag,
    )


def turned(pair, half):
    return jnp.concatenate([-pair[:, half:], pair[:, :half]], axis=1)


def wait_bytes(ref, sem):
    pltpu.make_async_copy(ref, ref, sem).wait()


def kernel(
    dims,
    hist_ref,
    row_ref,
    coup_ref,
    inv_ref,
    start_ref,
    time_ref,
    out_ref,
    h2,
    ebuf,
    vbuf,
    onehot,
    sendb,
    recvb,
    sendy,
    recvy,
    zown,
    sendz,
    recvz,
    hist_sem,
    v_send,
    v_recv,
    a_send,
    a_recv,
    b_send,
    b_recv,
    y_send,
    y_recv,
    z_send,
    z_recv,
):
    n_hist, n_second, n_y, order, cuts, steps = dims
    n_z = n_hist // n_y
    own, slab, width = row_ref.shape
    half = width // 4
    pair = 2 * half
    slots = time_ref.shape[0]
    times = ebuf.shape[1]
    rows = own * 2 * slab
    h = lax.axis_index("hist")
    sec = lax.axis_index("second")
    z = h // n_y
    y = lax.rem(h, n_y)

    def hist_peer(d):
        return lax.rem(h + d, n_hist)

    def second_peer(d):
        return lax.rem(sec + d, n_second)

    barrier = pltpu.get_barrier_semaphore()

    @pl.loop(1, n_second)
    def _(d):
        pl.semaphore_signal(barrier, 1, device_id=(h, second_peer(d)), device_id_type=MESH)

    @pl.loop(1, n_hist)
    def _(d):
        pl.semaphore_signal(barrier, 1, device_id=(hist_peer(d), sec), device_id_type=MESH)

    load_hist = pltpu.make_async_copy(hist_ref, h2, hist_sem)
    load_hist.start()

    anchor = start_ref[0].astype(F32)
    row8 = lax.broadcasted_iota(jnp.int32, (8, times), 0)
    tile = jnp.full((8, times), -1.0, F32)
    for s in range(slots):
        held = time_ref[s].astype(F32)
        tile = jnp.where(lax.rem(row8, slots) == s, held, tile)
    vbuf[h] = tile

    weight_sq = coup_ref[...] * coup_ref[...]

    def put_energy(w, green):
        for b in range(own):
            less, more = green[b][0], green[b][1]
            lr, li, mr, mi = less[:, :half], less[:, half:], more[:, :half], more[:, half:]
            less_r, less_i = cubic_term(lr, li, mr, mi)
            more_r, more_i = cubic_term(mr, mi, lr, li)
            weight = weight_sq[b : b + 1, :]
            both = jnp.concatenate([weight * (more_r - less_r), weight * (more_i - less_i)], axis=1)
            ebuf[w, pl.ds(pl.multiple_of(sec * slab, slab), slab), b * pair : (b + 1) * pair] = both.astype(BF16)

    def send_energy(w):
        mine = ebuf.at[w, pl.ds(pl.multiple_of(sec * slab, slab), slab)]

        @pl.loop(1, n_second)
        def _(d):
            pltpu.make_async_remote_copy(
                mine, mine, a_send.at[w], a_recv.at[w], device_id=(h, second_peer(d)), device_id_type=MESH
            ).start()

    green = [[row_ref[b, :, m * pair : (m + 1) * pair] for m in range(2)] for b in range(own)]
    put_energy(0, green)

    pl.semaphore_wait(barrier, n_second - 1 + n_hist - 1)
    send_energy(0)

    @pl.loop(1, n_hist)
    def _(d):
        pltpu.make_async_remote_copy(
            vbuf.at[h], vbuf.at[h], v_send, v_recv, device_id=(hist_peer(d), sec), device_id_type=MESH
        ).start()

    wait_bytes(vbuf.at[0 : n_hist - 1], v_recv)
    asked = vbuf[...].reshape(n_hist * 8, times)
    lane = lax.broadcasted_iota(jnp.int32, (n_hist * 8, times), 1).astype(F32)
    onehot[0 : n_hist * 8, :] = jnp.where((asked == lane) & (asked <= anchor), 1.0, 0.0).astype(BF16)
    row16 = lax.broadcasted_iota(jnp.int32, (16, times), 0)
    lane16 = lax.broadcasted_iota(jnp.int32, (16, times), 1).astype(F32)
    later = anchor + 1.0 + lax.rem(row16, 2).astype(F32)
    onehot[n_hist * 8 : n_hist * 8 + 16, :] = jnp.where((later == lane16) & (row16 < 2 * own), 1.0, 0.0).astype(BF16)

    past = []
    for w in range(steps):
        wait_bytes(ebuf.at[w, 0 : times - slab], a_recv.at[w])
        picked = jnp.dot(onehot[...], ebuf[w], preferred_element_type=F32)
        sub = lax.rem(lax.broadcasted_iota(jnp.int32, (n_hist * 8, pair), 0), 8)
        chosen = jnp.where(sub < slots, picked[: n_hist * 8, :pair], picked[: n_hist * 8, pair:])
        sub8 = lax.broadcasted_iota(jnp.int32, (8, pair), 0)
        extra = picked[n_hist * 8 : n_hist * 8 + 8]
        extra = jnp.where(sub8 < 2, extra[:, :pair], extra[:, pair:])
        piece = jnp.concatenate(
            [chosen.reshape(n_hist, 8, pair), jnp.broadcast_to(extra[None], (n_hist, 8, pair))], axis=1
        )
        sendb[w] = piece.astype(BF16)

        @pl.loop(1, n_hist)
        def _(d, w=w):
            to = hist_peer(d)
            pltpu.make_async_remote_copy(
                sendb.at[w, to], recvb.at[w, h], b_send.at[w], b_recv.at[w], device_id=(to, sec), device_id_type=MESH
            ).start()

        recvb[w, h] = sendb[w, h]
        wait_bytes(recvb.at[w, 0 : n_hist - 1], b_recv.at[w])
        got = recvb[w].astype(F32)
        left = got[:, :8].reshape(n_hist * 8, pair)
        weights = jnp.concatenate([left, turned(left, half)], axis=0).astype(BF16)
        if w == 0:
            load_hist.wait()

        def product(off, first, last):
            to_y = lax.rem(y + off, n_y)
            block = jnp.concatenate([h2[lax.rem(z + order[n], n_z), to_y] for n in range(first, last)], axis=0)
            return jnp.dot(block, weights, preferred_element_type=F32).reshape(last - first, rows, pair)

        for c, (first, last) in enumerate(cuts):
            for off in sorted(range(1, n_y), key=lambda o: -min(o, n_y - o)):
                sendy[w, off - 1, first:last] = product(off, first, last).astype(BF16)
                part = (w, off - 1, pl.ds(first, last - first))
                pltpu.make_async_remote_copy(
                    sendy.at[part],
                    recvy.at[part],
                    y_send.at[w],
                    y_recv.at[w, c],
                    device_id=(z * n_y + lax.rem(y + off, n_y), sec),
                    device_id_type=MESH,
                ).start()
        for first, last in cuts:
            zown[first:last] = product(0, first, last)

        local = [[green[b][m] for m in range(2)] for b in range(own)]
        recent = None
        if w:
            tail = got[:, 8:].reshape(n_hist * 8, pair).astype(BF16)
            rec = [None] * w
            for i in range(w):
                orbital = lax.broadcasted_iota(jnp.int32, (half, n_hist * 8), 0)
                at = lax.broadcasted_iota(jnp.int32, (half, n_hist * 8), 1)
                pick = jnp.where(at == (orbital // own) * 8 + lax.rem(orbital, own) * 2 + i, 1.0, 0.0).astype(BF16)
                column = jnp.dot(pick, tail, preferred_element_type=F32)
                matrix = jnp.concatenate([column, turned(column, half)], axis=0)
                rec[i] = jnp.dot(past[i], matrix, precision=HIGHEST, preferred_element_type=F32)
            recent = rec[0] if w == 1 else rec[0] + rec[1]

        total = None
        for c, (first, last) in enumerate(cuts):
            wait_bytes(recvy.at[w, :, first:last], y_recv.at[w, c])
            for n in range(first, last):
                acc = zown[n]
                for k in range(n_y - 1):
                    acc = acc + recvy[w, k, n].astype(F32)
                if order[n] == 0:
                    total = acc
                    continue
                sendz[w, n] = acc.astype(BF16)
                pltpu.make_async_remote_copy(
                    sendz.at[w, n],
                    recvz.at[w, n],
                    z_send.at[w],
                    z_recv.at[w],
                    device_id=(lax.rem(z + order[n], n_z) * n_y + y, sec),
                    device_id_type=MESH,
                ).start()
        wait_bytes(recvz.at[w], z_recv.at[w])
        for n in range(n_z - 1):
            total = total + recvz[w, n].astype(F32)
        if recent is not None:
            total = total + recent

        current = jnp.concatenate([local[b][m] for b in range(own) for m in range(2)], axis=0)
        moved = current + STEP_WIDTH * total
        real, imag = inv_ref[w, 0], inv_ref[w, 1]
        advance = jnp.concatenate(
            [jnp.concatenate([real, -imag], axis=1), jnp.concatenate([imag, real], axis=1)], axis=0
        )
        new = lax.dot_general(
            moved, advance, (((1,), (1,)), ((), ())), precision=HIGHEST, preferred_element_type=F32
        )
        past.append(new)
        split = new.reshape(own, 2, slab, pair)
        green = [[split[b, m] for m in range(2)] for b in range(own)]
        if w + 1 < steps:
            put_energy(w + 1, green)
            send_energy(w + 1)
        else:
            for b in range(own):
                for m in range(2):
                    out_ref[b, :, m * pair : (m + 1) * pair] = green[b][m]

    wait_bytes(vbuf.at[0 : n_hist - 1], v_send)
    for w in range(steps):
        wait_bytes(ebuf.at[w, 0 : times - slab], a_send.at[w])
        wait_bytes(recvb.at[w, 0 : n_hist - 1], b_send.at[w])
        wait_bytes(recvy.at[w], y_send.at[w])
        wait_bytes(recvz.at[w], z_send.at[w])


def body(n_hist, n_second, n_y, history, row_now, coupling, step_inverse, start_step, history_time):
    slots, orbitals, slab = history.shape[:3]
    own = row_now.shape[0]
    pair = 2 * orbitals
    n_z = n_hist // n_y
    steps = step_inverse.shape[0]
    times = slab * n_second
    rows = own * 2 * slab
    order = sorted(range(n_z), key=lambda d: (-min(d, n_z - d), d))
    cuts = ((0, n_z // 2), (n_z // 2, n_z))
    dims = (n_hist, n_second, n_y, tuple(order), cuts, steps)
    blocks = history.reshape(slots, orbitals, slab, 2, orbitals, 2)
    blocks = blocks.transpose(4, 3, 2, 5, 1, 0).reshape(n_z, n_y, rows, 2 * orbitals * slots)
    vmem = pl.BlockSpec(memory_space=pltpu.VMEM)
    smem = pl.BlockSpec(memory_space=pltpu.SMEM)
    dma = pltpu.SemaphoreType.DMA
    return pl.pallas_call(
        functools.partial(kernel, dims),
        out_shape=jax.ShapeDtypeStruct(row_now.shape, F32),
        in_specs=[pl.BlockSpec(memory_space=pl.ANY), vmem, vmem, vmem, smem, smem],
        out_specs=vmem,
        scratch_shapes=[
            pltpu.VMEM(blocks.shape, BF16),
            pltpu.VMEM((steps, times, own * pair), BF16),
            pltpu.VMEM((n_hist, 8, times), F32),
            pltpu.VMEM((n_hist * 8 + 16, times), BF16),
            pltpu.VMEM((steps, n_hist, 16, pair), BF16),
            pltpu.VMEM((steps, n_hist, 16, pair), BF16),
            pltpu.VMEM((steps, n_y - 1, n_z, rows, pair), BF16),
            pltpu.VMEM((steps, n_y - 1, n_z, rows, pair), BF16),
            pltpu.VMEM((n_z, rows, pair), F32),
            pltpu.VMEM((steps, n_z - 1, rows, pair), BF16),
            pltpu.VMEM((steps, n_z - 1, rows, pair), BF16),
            dma,
            dma,
            dma,
            dma((steps,)),
            dma((steps,)),
            dma((steps,)),
            dma((steps,)),
            dma((steps,)),
            dma((steps, len(cuts))),
            dma((steps,)),
            dma((steps,)),
        ],
        compiler_params=pltpu.CompilerParams(
            collective_id=0, has_side_effects=True, vmem_limit_bytes=32 * 1024 * 1024
        ),
    )(blocks, row_now, coupling, step_inverse, start_step, history_time)


def solution(mesh):
    placed = (
        P("hist", None, "second", None, None),
        P("hist", "second", None),
        P("hist", None),
        P(),
        P(),
        P("hist"),
    )
    return jax.shard_map(
        functools.partial(body, mesh.shape["hist"], mesh.shape["second"], CHIPS_Y),
        mesh=mesh,
        in_specs=placed,
        out_specs=P("hist", "second", None),
        check_vma=False,
    )
```

```python
import functools

import jax
import jax.numpy as jnp
from jax import lax
from jax.experimental import pallas as pl
from jax.experimental.pallas import tpu as pltpu
from jax.sharding import PartitionSpec as P

MESH = pl.DeviceIdType.MESH
HIGHEST = lax.Precision.HIGHEST
STEP_WIDTH = 0.05
CHIPS_Y = 4
F32 = jnp.float32
BF16 = jnp.bfloat16


def cubic_term(first_real, first_imag, other_real, other_imag):
    square_real = first_real * first_real - first_imag * first_imag
    square_imag = 2.0 * first_real * first_imag
    return (
        square_real * other_real + square_imag * other_imag,
        square_imag * other_real - square_real * other_imag,
    )


def turned(pair, half):
    return jnp.concatenate([-pair[:, half:], pair[:, :half]], axis=1)


def wait_bytes(ref, sem):
    pltpu.make_async_copy(ref, ref, sem).wait()


def kernel(
    dims,
    hist_ref,
    row_ref,
    coup_ref,
    inv_ref,
    start_ref,
    time_ref,
    out_ref,
    stored,
    spread,
    h2,
    ebuf,
    vbuf,
    onehot,
    sendb,
    recvb,
    sendy,
    recvy,
    zown,
    summed,
    sendz,
    recvz,
    hist_sem,
    v_send,
    v_recv,
    a_send,
    a_recv,
    b_send,
    b_recv,
    y_send,
    y_recv,
    z_send,
    z_recv,
):
    n_hist, n_second, n_y, order, cuts, steps = dims
    n_z = n_hist // n_y
    own, slab, width = row_ref.shape
    half = width // 4
    pair = 2 * half
    slots = time_ref.shape[0]
    times = ebuf.shape[1]
    rows = own * 2 * slab
    h = lax.axis_index("hist")
    sec = lax.axis_index("second")
    z = h // n_y
    y = lax.rem(h, n_y)

    def hist_peer(d):
        return lax.rem(h + d, n_hist)

    def second_peer(d):
        return lax.rem(sec + d, n_second)

    barrier = pltpu.get_barrier_semaphore()

    @pl.loop(1, n_second)
    def _(d):
        pl.semaphore_signal(barrier, 1, device_id=(h, second_peer(d)), device_id_type=MESH)

    @pl.loop(1, n_hist)
    def _(d):
        pl.semaphore_signal(barrier, 1, device_id=(hist_peer(d), sec), device_id_type=MESH)

    load_hist = pltpu.make_async_copy(hist_ref, stored, hist_sem)
    load_hist.start()

    anchor = start_ref[0].astype(F32)
    row8 = lax.broadcasted_iota(jnp.int32, (8, times), 0)
    tile = jnp.full((8, times), -1.0, F32)
    for s in range(slots):
        held = time_ref[s].astype(F32)
        tile = jnp.where(lax.rem(row8, slots) == s, held, tile)
    vbuf[h] = tile

    weight_sq = coup_ref[...] * coup_ref[...]

    def put_energy(w, green):
        for b in range(own):
            less, more = green[b][0], green[b][1]
            lr, li, mr, mi = less[:, :half], less[:, half:], more[:, :half], more[:, half:]
            less_r, less_i = cubic_term(lr, li, mr, mi)
            more_r, more_i = cubic_term(mr, mi, lr, li)
            weight = weight_sq[b : b + 1, :]
            both = jnp.concatenate([weight * (more_r - less_r), weight * (more_i - less_i)], axis=1)
            ebuf[w, pl.ds(pl.multiple_of(sec * slab, slab), slab), b * pair : (b + 1) * pair] = both.astype(BF16)

    def send_energy(w):
        mine = ebuf.at[w, pl.ds(pl.multiple_of(sec * slab, slab), slab)]

        @pl.loop(1, n_second)
        def _(d):
            pltpu.make_async_remote_copy(
                mine, mine, a_send.at[w], a_recv.at[w], device_id=(h, second_peer(d)), device_id_type=MESH
            ).start()

    green = [[row_ref[b, :, m * pair : (m + 1) * pair] for m in range(2)] for b in range(own)]
    put_energy(0, green)

    pl.semaphore_wait(barrier, n_second - 1 + n_hist - 1)
    send_energy(0)

    @pl.loop(1, n_hist)
    def _(d):
        pltpu.make_async_remote_copy(
            vbuf.at[h], vbuf.at[h], v_send, v_recv, device_id=(hist_peer(d), sec), device_id_type=MESH
        ).start()

    load_hist.wait()
    wide = 2 * slab

    @pl.loop(0, half)
    def _(j):
        for s in range(slots):
            at = pl.multiple_of((j * slots + s) * wide, wide)
            spread[pl.ds(at, wide), :] = stored[pl.ds(pl.multiple_of((s * half + j) * wide, wide), wide), :].astype(F32)

    index = lax.broadcasted_iota(jnp.int32, (pair, pair), 0)
    place = lax.rem(index // own, n_z)
    depth = jnp.zeros_like(index)
    for n in range(n_z):
        depth = jnp.where(place == n, lax.rem(z + order[n], n_z), depth)
    to_y = lax.rem(lax.rem(index // (own * n_z), n_y) + y, n_y)
    column = ((depth * n_y + to_y) * own + lax.rem(index, own)) * 2 + index // half
    turn = jnp.where(lax.broadcasted_iota(jnp.int32, (pair, pair), 1) == column, 1.0, 0.0).astype(BF16)
    depth_of = half * slots
    unit = (n_z // len(cuts)) * own

    @pl.loop(0, slab // 2)
    def _(u):
        for m in range(2):
            both = []
            for k in range(2):
                block = spread[pl.ds((2 * u + k) * 2 + m, depth_of, stride=wide), :].astype(BF16)
                both.append(
                    lax.dot_general(turn, block, (((1,), (1,)), ((), ())), preferred_element_type=F32)
                )
            for p in range(2):
                for off in range(n_y):
                    for c in range(len(cuts)):
                        at = p * half + (off * len(cuts) + c) * unit
                        h2[
                            off,
                            c,
                            pl.ds(pl.multiple_of((m * slab + 2 * u) * unit, 2 * unit), 2 * unit),
                            p * depth_of : (p + 1) * depth_of,
                        ] = jnp.concatenate([one[at : at + unit] for one in both], axis=0).astype(BF16)

    wait_bytes(vbuf.at[0 : n_hist - 1], v_recv)
    asked = vbuf[...].reshape(n_hist * 8, times)
    lane = lax.broadcasted_iota(jnp.int32, (n_hist * 8, times), 1).astype(F32)
    onehot[0 : n_hist * 8, :] = jnp.where((asked == lane) & (asked <= anchor), 1.0, 0.0).astype(BF16)
    row16 = lax.broadcasted_iota(jnp.int32, (16, times), 0)
    lane16 = lax.broadcasted_iota(jnp.int32, (16, times), 1).astype(F32)
    later = anchor + 1.0 + lax.rem(row16, 2).astype(F32)
    onehot[n_hist * 8 : n_hist * 8 + 16, :] = jnp.where((later == lane16) & (row16 < 2 * own), 1.0, 0.0).astype(BF16)

    past = []
    for w in range(steps):
        wait_bytes(ebuf.at[w, 0 : times - slab], a_recv.at[w])
        picked = jnp.dot(onehot[...], ebuf[w], preferred_element_type=F32)
        sub = lax.rem(lax.broadcasted_iota(jnp.int32, (n_hist * 8, pair), 0), 8)
        chosen = jnp.where(sub < slots, picked[: n_hist * 8, :pair], picked[: n_hist * 8, pair:])
        sub8 = lax.broadcasted_iota(jnp.int32, (8, pair), 0)
        extra = picked[n_hist * 8 : n_hist * 8 + 8]
        extra = jnp.where(sub8 < 2, extra[:, :pair], extra[:, pair:])
        piece = jnp.concatenate(
            [chosen.reshape(n_hist, 8, pair), jnp.broadcast_to(extra[None], (n_hist, 8, pair))], axis=1
        )
        sendb[w] = piece.astype(BF16)

        @pl.loop(1, n_hist)
        def _(d, w=w):
            to = hist_peer(d)
            pltpu.make_async_remote_copy(
                sendb.at[w, to], recvb.at[w, h], b_send.at[w], b_recv.at[w], device_id=(to, sec), device_id_type=MESH
            ).start()

        recvb[w, h] = sendb[w, h]
        wait_bytes(recvb.at[w, 0 : n_hist - 1], b_recv.at[w])
        got = recvb[w].astype(F32)
        left = got[:, :8].reshape(n_hist * 8, pair)
        weights = jnp.concatenate([left, turned(left, half)], axis=0).astype(BF16)

        def product(off, c):
            return jnp.dot(h2[off, c], weights, preferred_element_type=F32)

        for c in range(len(cuts)):
            for off in sorted(range(1, n_y), key=lambda o: -min(o, n_y - o)):
                sendy[w, c, off - 1] = product(off, c).astype(BF16)
                pltpu.make_async_remote_copy(
                    sendy.at[w, c, off - 1],
                    recvy.at[w, c, off - 1],
                    y_send.at[w],
                    y_recv.at[w, c],
                    device_id=(z * n_y + lax.rem(y + off, n_y), sec),
                    device_id_type=MESH,
                ).start()
        for c in range(len(cuts)):
            zown[c] = product(0, c)

        local = [[green[b][m] for m in range(2)] for b in range(own)]
        recent = None
        if w:
            tail = got[:, 8:].reshape(n_hist * 8, pair).astype(BF16)
            rec = [None] * w
            for i in range(w):
                orbital = lax.broadcasted_iota(jnp.int32, (half, n_hist * 8), 0)
                at = lax.broadcasted_iota(jnp.int32, (half, n_hist * 8), 1)
                pick = jnp.where(at == (orbital // own) * 8 + lax.rem(orbital, own) * 2 + i, 1.0, 0.0).astype(BF16)
                column = jnp.dot(pick, tail, preferred_element_type=F32)
                matrix = jnp.concatenate([column, turned(column, half)], axis=0)
                rec[i] = jnp.dot(past[i], matrix, precision=HIGHEST, preferred_element_type=F32)
            recent = rec[0] if w == 1 else rec[0] + rec[1]

        total = None
        for c, (first, last) in enumerate(cuts):
            wait_bytes(recvy.at[w, c], y_recv.at[w, c])
            acc = zown[c]
            for k in range(n_y - 1):
                acc = acc + recvy[w, c, k].astype(F32)
            summed[c] = acc
            for n in range(first, last):
                acc = jnp.concatenate(
                    [summed[c, pl.ds((n - first) * own + b, wide, stride=unit), :] for b in range(own)], axis=0
                )
                if order[n] == 0:
                    total = acc
                    continue
                sendz[w, n] = acc.astype(BF16)
                pltpu.make_async_remote_copy(
                    sendz.at[w, n],
                    recvz.at[w, n],
                    z_send.at[w],
                    z_recv.at[w],
                    device_id=(lax.rem(z + order[n], n_z) * n_y + y, sec),
                    device_id_type=MESH,
                ).start()
        wait_bytes(recvz.at[w], z_recv.at[w])
        for n in range(n_z - 1):
            total = total + recvz[w, n].astype(F32)
        if recent is not None:
            total = total + recent

        current = jnp.concatenate([local[b][m] for b in range(own) for m in range(2)], axis=0)
        moved = current + STEP_WIDTH * total
        real, imag = inv_ref[w, 0], inv_ref[w, 1]
        advance = jnp.concatenate(
            [jnp.concatenate([real, -imag], axis=1), jnp.concatenate([imag, real], axis=1)], axis=0
        )
        new = lax.dot_general(
            moved, advance, (((1,), (1,)), ((), ())), precision=HIGHEST, preferred_element_type=F32
        )
        past.append(new)
        split = new.reshape(own, 2, slab, pair)
        green = [[split[b, m] for m in range(2)] for b in range(own)]
        if w + 1 < steps:
            put_energy(w + 1, green)
            send_energy(w + 1)
        else:
            for b in range(own):
                for m in range(2):
                    out_ref[b, :, m * pair : (m + 1) * pair] = green[b][m]

    wait_bytes(vbuf.at[0 : n_hist - 1], v_send)
    for w in range(steps):
        wait_bytes(ebuf.at[w, 0 : times - slab], a_send.at[w])
        wait_bytes(recvb.at[w, 0 : n_hist - 1], b_send.at[w])
        wait_bytes(recvy.at[w], y_send.at[w])
        wait_bytes(recvz.at[w], z_send.at[w])


def body(n_hist, n_second, n_y, history, row_now, coupling, step_inverse, start_step, history_time):
    slots, orbitals, slab = history.shape[:3]
    own = row_now.shape[0]
    pair = 2 * orbitals
    n_z = n_hist // n_y
    steps = step_inverse.shape[0]
    times = slab * n_second
    rows = own * 2 * slab
    order = sorted(range(n_z), key=lambda d: (-min(d, n_z - d), d))
    cuts = ((0, n_z // 2), (n_z // 2, n_z))
    dims = (n_hist, n_second, n_y, tuple(order), cuts, steps)
    part = rows * n_z // len(cuts)
    blocks = history.reshape(slots * orbitals * slab * 2, pair)
    vmem = pl.BlockSpec(memory_space=pltpu.VMEM)
    smem = pl.BlockSpec(memory_space=pltpu.SMEM)
    dma = pltpu.SemaphoreType.DMA
    return pl.pallas_call(
        functools.partial(kernel, dims),
        out_shape=jax.ShapeDtypeStruct(row_now.shape, F32),
        in_specs=[pl.BlockSpec(memory_space=pl.ANY), vmem, vmem, vmem, smem, smem],
        out_specs=vmem,
        scratch_shapes=[
            pltpu.VMEM(blocks.shape, BF16),
            pltpu.VMEM(blocks.shape, F32),
            pltpu.VMEM((n_y, len(cuts), part, pair * slots), BF16),
            pltpu.VMEM((steps, times, own * pair), BF16),
            pltpu.VMEM((n_hist, 8, times), F32),
            pltpu.VMEM((n_hist * 8 + 16, times), BF16),
            pltpu.VMEM((steps, n_hist, 16, pair), BF16),
            pltpu.VMEM((steps, n_hist, 16, pair), BF16),
            pltpu.VMEM((steps, len(cuts), n_y - 1, part, pair), BF16),
            pltpu.VMEM((steps, len(cuts), n_y - 1, part, pair), BF16),
            pltpu.VMEM((len(cuts), part, pair), F32),
            pltpu.VMEM((len(cuts), part, pair), F32),
            pltpu.VMEM((steps, n_z - 1, rows, pair), BF16),
            pltpu.VMEM((steps, n_z - 1, rows, pair), BF16),
            dma,
            dma,
            dma,
            dma((steps,)),
            dma((steps,)),
            dma((steps,)),
            dma((steps,)),
            dma((steps,)),
            dma((steps, len(cuts))),
            dma((steps,)),
            dma((steps,)),
        ],
        compiler_params=pltpu.CompilerParams(
            collective_id=0, has_side_effects=True, vmem_limit_bytes=32 * 1024 * 1024
        ),
    )(blocks, row_now, coupling, step_inverse, start_step, history_time)


def solution(mesh):
    placed = (
        P("hist", None, "second", None, None),
        P("hist", "second", None),
        P("hist", None),
        P(),
        P(),
        P("hist"),
    )
    return jax.shard_map(
        functools.partial(body, mesh.shape["hist"], mesh.shape["second"], CHIPS_Y),
        mesh=mesh,
        in_specs=placed,
        out_specs=P("hist", "second", None),
        check_vma=False,
    )
```

```python
import functools

import jax
import jax.numpy as jnp
from jax import lax
from jax.experimental import pallas as pl
from jax.experimental.pallas import tpu as pltpu
from jax.sharding import PartitionSpec as P

MESH = pl.DeviceIdType.MESH
HIGHEST = lax.Precision.HIGHEST
STEP_WIDTH = 0.05
CHIPS_Y = 4
F32 = jnp.float32
BF16 = jnp.bfloat16


def cubic_term(first_real, first_imag, other_real, other_imag):
    square_real = first_real * first_real - first_imag * first_imag
    square_imag = 2.0 * first_real * first_imag
    return (
        square_real * other_real + square_imag * other_imag,
        square_imag * other_real - square_real * other_imag,
    )


def turned(pair, half):
    return jnp.concatenate([-pair[:, half:], pair[:, :half]], axis=1)


def wait_bytes(ref, sem):
    pltpu.make_async_copy(ref, ref, sem).wait()


def kernel(
    dims,
    hist_hbm,
    row_hbm,
    coup_hbm,
    inv_hbm,
    start_hbm,
    time_hbm,
    out_ref,
    row_ref,
    coup_ref,
    inv_ref,
    start_ref,
    time_ref,
    stored,
    spread,
    h2,
    ebuf,
    vbuf,
    onehot,
    sendb,
    recvb,
    sendy,
    recvy,
    zown,
    summed,
    sendz,
    recvz,
    in_sem,
    v_send,
    v_recv,
    a_send,
    a_recv,
    b_send,
    b_recv,
    y_send,
    y_recv,
    z_send,
    z_recv,
):
    n_hist, n_second, n_y, order, cuts, steps = dims
    n_z = n_hist // n_y
    own, slab, width = row_ref.shape
    half = width // 4
    pair = 2 * half
    slots = time_ref.shape[0]
    times = ebuf.shape[1]
    rows = own * 2 * slab
    h = lax.axis_index("hist")
    sec = lax.axis_index("second")
    z = h // n_y
    y = lax.rem(h, n_y)

    def outward(k, n):
        step = (k + 1) // 2
        return n // 2 + step - 2 * step * lax.rem(k, 2)

    def hist_peer(k):
        return lax.rem(z + outward(k // n_y, n_z), n_z) * n_y + lax.rem(y + outward(lax.rem(k, n_y), n_y), n_y)

    def second_peer(k):
        x = lax.rem(sec // 2 + outward(k // 2, n_second // 2), n_second // 2)
        return x * 2 + lax.rem(lax.rem(sec, 2) + 1 - lax.rem(k, 2), 2)

    barrier = pltpu.get_barrier_semaphore()

    @pl.loop(0, n_hist - 1)
    def _(k):
        pl.semaphore_signal(barrier, 1, device_id=(hist_peer(k), sec), device_id_type=MESH)

    @pl.loop(0, n_second - 1)
    def _(k):
        pl.semaphore_signal(barrier, 1, device_id=(h, second_peer(k)), device_id_type=MESH)

    loads = [
        pltpu.make_async_copy(src, dst, in_sem.at[i])
        for i, (src, dst) in enumerate(
            (
                (start_hbm, start_ref),
                (time_hbm, time_ref),
                (coup_hbm, coup_ref),
                (row_hbm, row_ref),
                (hist_hbm, stored),
                (inv_hbm, inv_ref),
            )
        )
    ]
    for load in loads:
        load.start()
    for load in loads[:4]:
        load.wait()

    anchor = start_ref[0].astype(F32)
    row8 = lax.broadcasted_iota(jnp.int32, (8, times), 0)
    tile = jnp.full((8, times), -1.0, F32)
    for s in range(slots):
        held = time_ref[s].astype(F32)
        tile = jnp.where(lax.rem(row8, slots) == s, held, tile)
    vbuf[h] = tile

    weight_sq = coup_ref[...] * coup_ref[...]

    def put_energy(w, green):
        for b in range(own):
            less, more = green[b][0], green[b][1]
            lr, li, mr, mi = less[:, :half], less[:, half:], more[:, :half], more[:, half:]
            less_r, less_i = cubic_term(lr, li, mr, mi)
            more_r, more_i = cubic_term(mr, mi, lr, li)
            weight = weight_sq[b : b + 1, :]
            both = jnp.concatenate([weight * (more_r - less_r), weight * (more_i - less_i)], axis=1)
            ebuf[w, pl.ds(pl.multiple_of(sec * slab, slab), slab), b * pair : (b + 1) * pair] = both.astype(BF16)

    def send_energy(w):
        mine = ebuf.at[w, pl.ds(pl.multiple_of(sec * slab, slab), slab)]

        @pl.loop(0, n_second - 1)
        def _(k):
            pltpu.make_async_remote_copy(
                mine, mine, a_send.at[w], a_recv.at[w], device_id=(h, second_peer(k)), device_id_type=MESH
            ).start()

    part = 2 * slab * (n_z // len(cuts)) * own
    green = [[row_ref[b, :, m * pair : (m + 1) * pair] for m in range(2)] for b in range(own)]
    put_energy(0, green)

    wide = 2 * slab
    loads[4].wait()

    @pl.loop(0, half)
    def _(j):
        for s in range(slots):
            at = pl.multiple_of((j * slots + s) * wide, wide)
            spread[pl.ds(at, wide), :] = stored[pl.ds(pl.multiple_of((s * half + j) * wide, wide), wide), :].astype(F32)

    pl.semaphore_wait(barrier, n_second - 1 + n_hist - 1)

    @pl.loop(0, n_hist - 1)
    def _(k):
        pltpu.make_async_remote_copy(
            vbuf.at[h], vbuf.at[h], v_send, v_recv, device_id=(hist_peer(k), sec), device_id_type=MESH
        ).start()

    send_energy(0)

    index = lax.broadcasted_iota(jnp.int32, (pair, pair), 0)
    place = lax.rem(index // own, n_z)
    depth = jnp.zeros_like(index)
    for n in range(n_z):
        depth = jnp.where(place == n, lax.rem(z + order[n], n_z), depth)
    to_y = lax.rem(lax.rem(index // (own * n_z), n_y) + y, n_y)
    column = ((depth * n_y + to_y) * own + lax.rem(index, own)) * 2 + index // half
    turn = jnp.where(lax.broadcasted_iota(jnp.int32, (pair, pair), 1) == column, 1.0, 0.0).astype(BF16)
    depth_of = half * slots
    unit = (n_z // len(cuts)) * own

    @pl.loop(0, slab // 2)
    def _(u):
        for m in range(2):
            both = []
            for k in range(2):
                block = spread[pl.ds((2 * u + k) * 2 + m, depth_of, stride=wide), :].astype(BF16)
                both.append(
                    lax.dot_general(turn, block, (((1,), (1,)), ((), ())), preferred_element_type=F32)
                )
            for p in range(2):
                for off in range(n_y):
                    for c in range(len(cuts)):
                        at = p * half + (off * len(cuts) + c) * unit
                        h2[
                            c,
                            off,
                            pl.ds(pl.multiple_of((m * slab + 2 * u) * unit, 2 * unit), 2 * unit),
                            p * depth_of : (p + 1) * depth_of,
                        ] = jnp.concatenate([one[at : at + unit] for one in both], axis=0).astype(BF16)

    wait_bytes(vbuf.at[0 : n_hist - 1], v_recv)
    asked = vbuf[...].reshape(n_hist * 8, times)
    lane = lax.broadcasted_iota(jnp.int32, (n_hist * 8, times), 1).astype(F32)
    onehot[0 : n_hist * 8, :] = jnp.where((asked == lane) & (asked <= anchor), 1.0, 0.0).astype(BF16)
    row16 = lax.broadcasted_iota(jnp.int32, (16, times), 0)
    lane16 = lax.broadcasted_iota(jnp.int32, (16, times), 1).astype(F32)
    later = anchor + 1.0 + lax.rem(row16, 2).astype(F32)
    onehot[n_hist * 8 : n_hist * 8 + 16, :] = jnp.where((later == lane16) & (row16 < 2 * own), 1.0, 0.0).astype(BF16)

    loads[5].wait()
    past = []
    for w in range(steps):
        wait_bytes(ebuf.at[w, 0 : times - slab], a_recv.at[w])
        picked = jnp.dot(onehot[...], ebuf[w], preferred_element_type=F32)
        sub = lax.rem(lax.broadcasted_iota(jnp.int32, (n_hist * 8, pair), 0), 8)
        chosen = jnp.where(sub < slots, picked[: n_hist * 8, :pair], picked[: n_hist * 8, pair:])
        sub8 = lax.broadcasted_iota(jnp.int32, (8, pair), 0)
        extra = picked[n_hist * 8 : n_hist * 8 + 8]
        extra = jnp.where(sub8 < 2, extra[:, :pair], extra[:, pair:])
        piece = jnp.concatenate(
            [chosen.reshape(n_hist, 8, pair), jnp.broadcast_to(extra[None], (n_hist, 8, pair))], axis=1
        )
        sendb[w] = piece.astype(BF16)

        @pl.loop(0, n_hist - 1)
        def _(k, w=w):
            to = hist_peer(k)
            pltpu.make_async_remote_copy(
                sendb.at[w, to], recvb.at[w, h], b_send.at[w], b_recv.at[w], device_id=(to, sec), device_id_type=MESH
            ).start()

        recvb[w, h] = sendb[w, h]
        wait_bytes(recvb.at[w, 0 : n_hist - 1], b_recv.at[w])
        got = recvb[w].astype(F32)
        left = got[:, :8].reshape(n_hist * 8, pair)
        weights = jnp.concatenate([left, turned(left, half)], axis=0).astype(BF16)

        for c in range(len(cuts)):
            product = jnp.dot(
                h2[c, 1:].reshape((n_y - 1) * part, pair * slots), weights, preferred_element_type=F32
            ).astype(BF16)
            for off in range(1, n_y):
                sendy[w, c, off - 1] = product[(off - 1) * part : off * part]
            for m in range(2):
                for off in sorted(range(1, n_y), key=lambda o: -min(o, n_y - o)):
                    own_m = (w, c, off - 1, pl.ds(m * part // 2, part // 2))
                    pltpu.make_async_remote_copy(
                        sendy.at[own_m],
                        recvy.at[own_m],
                        y_send.at[w],
                        y_recv.at[w, c, m],
                        device_id=(z * n_y + lax.rem(y + off, n_y), sec),
                        device_id_type=MESH,
                    ).start()
        for c in range(len(cuts)):
            zown[c] = jnp.dot(h2[c, 0], weights, preferred_element_type=F32)

        local = [[green[b][m] for m in range(2)] for b in range(own)]
        recent = None
        if w:
            tail = got[:, 8:].reshape(n_hist * 8, pair).astype(BF16)
            rec = [None] * w
            for i in range(w):
                orbital = lax.broadcasted_iota(jnp.int32, (half, n_hist * 8), 0)
                at = lax.broadcasted_iota(jnp.int32, (half, n_hist * 8), 1)
                pick = jnp.where(at == (orbital // own) * 8 + lax.rem(orbital, own) * 2 + i, 1.0, 0.0).astype(BF16)
                column = jnp.dot(pick, tail, preferred_element_type=F32)
                matrix = jnp.concatenate([column, turned(column, half)], axis=0)
                rec[i] = jnp.dot(past[i], matrix, precision=HIGHEST, preferred_element_type=F32)
            recent = rec[0] if w == 1 else rec[0] + rec[1]

        totals = [None, None]
        for c, (first, last) in enumerate(cuts):
            for m in range(2):
                of_m = pl.ds(m * part // 2, part // 2)
                wait_bytes(recvy.at[w, c, :, of_m], y_recv.at[w, c, m])
                acc = zown[c, of_m]
                for k in range(n_y - 1):
                    acc = acc + recvy[w, c, k, of_m].astype(F32)
                summed[c, of_m] = acc
                for n in range(first, last):
                    piece = jnp.concatenate(
                        [
                            summed[c, pl.ds(m * part // 2 + (n - first) * own + b, slab, stride=unit), :]
                            for b in range(own)
                        ],
                        axis=0,
                    )
                    if order[n] == 0:
                        totals[m] = piece
                        continue
                    sendz[w, n, m] = piece.astype(BF16)
                    pltpu.make_async_remote_copy(
                        sendz.at[w, n, m],
                        recvz.at[w, n, m],
                        z_send.at[w],
                        z_recv.at[w],
                        device_id=(lax.rem(z + order[n], n_z) * n_y + y, sec),
                        device_id_type=MESH,
                    ).start()
        wait_bytes(recvz.at[w], z_recv.at[w])
        for n in range(n_z - 1):
            totals = [totals[m] + recvz[w, n, m].astype(F32) for m in range(2)]
        total = jnp.concatenate(totals, axis=0)
        if recent is not None:
            total = total + recent

        current = jnp.concatenate([local[b][m] for m in range(2) for b in range(own)], axis=0)
        moved = current + STEP_WIDTH * total
        real, imag = inv_ref[w, 0], inv_ref[w, 1]
        advance = jnp.concatenate(
            [jnp.concatenate([real, -imag], axis=1), jnp.concatenate([imag, real], axis=1)], axis=0
        )
        new = lax.dot_general(
            moved, advance, (((1,), (1,)), ((), ())), precision=HIGHEST, preferred_element_type=F32
        )
        past.append(new)
        split = new.reshape(2, own, slab, pair)
        green = [[split[m, b] for m in range(2)] for b in range(own)]
        if w + 1 < steps:
            put_energy(w + 1, green)
            send_energy(w + 1)
        else:
            for b in range(own):
                for m in range(2):
                    out_ref[b, :, m * pair : (m + 1) * pair] = green[b][m]

    wait_bytes(vbuf.at[0 : n_hist - 1], v_send)
    for w in range(steps):
        wait_bytes(ebuf.at[w, 0 : times - slab], a_send.at[w])
        wait_bytes(recvb.at[w, 0 : n_hist - 1], b_send.at[w])
        wait_bytes(recvy.at[w], y_send.at[w])
        wait_bytes(recvz.at[w], z_send.at[w])


def body(n_hist, n_second, n_y, history, row_now, coupling, step_inverse, start_step, history_time):
    slots, orbitals, slab = history.shape[:3]
    own = row_now.shape[0]
    pair = 2 * orbitals
    n_z = n_hist // n_y
    steps = step_inverse.shape[0]
    times = slab * n_second
    rows = own * 2 * slab
    order = sorted(range(n_z), key=lambda d: (-min(d, n_z - d), d))
    cuts = ((0, n_z // 2), (n_z // 2, n_z))
    dims = (n_hist, n_second, n_y, tuple(order), cuts, steps)
    part = rows * n_z // len(cuts)
    blocks = history.reshape(slots * orbitals * slab * 2, pair)
    vmem = pl.BlockSpec(memory_space=pltpu.VMEM)
    dma = pltpu.SemaphoreType.DMA
    return pl.pallas_call(
        functools.partial(kernel, dims),
        out_shape=jax.ShapeDtypeStruct(row_now.shape, F32),
        in_specs=[pl.BlockSpec(memory_space=pltpu.HBM)] * 6,
        out_specs=vmem,
        scratch_shapes=[
            pltpu.VMEM(row_now.shape, F32),
            pltpu.VMEM(coupling.shape, F32),
            pltpu.VMEM(step_inverse.shape, F32),
            pltpu.SMEM(start_step.shape, jnp.int32),
            pltpu.SMEM(history_time.shape, jnp.int32),
            pltpu.VMEM(blocks.shape, BF16),
            pltpu.VMEM(blocks.shape, F32),
            pltpu.VMEM((len(cuts), n_y, part, pair * slots), BF16),
            pltpu.VMEM((steps, times, own * pair), BF16),
            pltpu.VMEM((n_hist, 8, times), F32),
            pltpu.VMEM((n_hist * 8 + 16, times), BF16),
            pltpu.VMEM((steps, n_hist, 16, pair), BF16),
            pltpu.VMEM((steps, n_hist, 16, pair), BF16),
            pltpu.VMEM((steps, len(cuts), n_y - 1, part, pair), BF16),
            pltpu.VMEM((steps, len(cuts), n_y - 1, part, pair), BF16),
            pltpu.VMEM((len(cuts), part, pair), F32),
            pltpu.VMEM((len(cuts), part, pair), F32),
            pltpu.VMEM((steps, n_z - 1, 2, own * slab, pair), BF16),
            pltpu.VMEM((steps, n_z - 1, 2, own * slab, pair), BF16),
            dma((6,)),
            dma,
            dma,
            dma((steps,)),
            dma((steps,)),
            dma((steps,)),
            dma((steps,)),
            dma((steps,)),
            dma((steps, len(cuts), 2)),
            dma((steps,)),
            dma((steps,)),
        ],
        compiler_params=pltpu.CompilerParams(
            collective_id=0, has_side_effects=True, vmem_limit_bytes=32 * 1024 * 1024
        ),
    )(blocks, row_now, coupling, step_inverse, start_step, history_time)


def solution(mesh):
    placed = (
        P("hist", None, "second", None, None),
        P("hist", "second", None),
        P("hist", None),
        P(),
        P(),
        P("hist"),
    )
    return jax.shard_map(
        functools.partial(body, mesh.shape["hist"], mesh.shape["second"], CHIPS_Y),
        mesh=mesh,
        in_specs=placed,
        out_specs=P("hist", "second", None),
        check_vma=False,
    )
```

```python
import functools

import jax
import jax.numpy as jnp
from jax import lax
from jax.experimental import pallas as pl
from jax.experimental.pallas import tpu as pltpu
from jax.sharding import PartitionSpec as P

MESH = pl.DeviceIdType.MESH
HIGHEST = lax.Precision.HIGHEST
STEP_WIDTH = 0.05
CHIPS_Y = 4
F32 = jnp.float32
BF16 = jnp.bfloat16


def cubic_term(first_real, first_imag, other_real, other_imag):
    square_real = first_real * first_real - first_imag * first_imag
    square_imag = 2.0 * first_real * first_imag
    return (
        square_real * other_real + square_imag * other_imag,
        square_imag * other_real - square_real * other_imag,
    )


def turned(pair, half):
    return jnp.concatenate([-pair[:, half:], pair[:, :half]], axis=1)


def wait_bytes(ref, sem):
    pltpu.make_async_copy(ref, ref, sem).wait()


def kernel(
    dims,
    hist_hbm,
    row_hbm,
    coup_hbm,
    inv_hbm,
    start_hbm,
    time_hbm,
    out_ref,
    row_ref,
    coup_ref,
    inv_ref,
    start_ref,
    time_ref,
    stored,
    spread,
    turned_hist,
    held,
    ebuf,
    vbuf,
    onehot,
    sendb,
    recvb,
    sendx,
    recvx,
    summed,
    sendz,
    recvz,
    in_sem,
    v_send,
    v_recv,
    a_send,
    a_recv,
    b_send,
    b_recv,
    x_send,
    x_recv,
    h_send,
    h_recv,
    z_send,
    z_recv,
):
    n_hist, n_second, n_y, order, steps = dims
    n_z = n_hist // n_y
    own, slab, width = row_ref.shape
    half = width // 4
    pair = 2 * half
    slots = time_ref.shape[0]
    times = ebuf.shape[1]
    rows = own * 2 * slab
    h = lax.axis_index("hist")
    sec = lax.axis_index("second")
    z = h // n_y
    y = lax.rem(h, n_y)

    def outward(k, n):
        step = (k + 1) // 2
        return n // 2 + step - 2 * step * lax.rem(k, 2)

    def hist_peer(k):
        return lax.rem(z + outward(k // n_y, n_z), n_z) * n_y + lax.rem(y + outward(lax.rem(k, n_y), n_y), n_y)

    def second_peer(k):
        x = lax.rem(sec // 2 + outward(k // 2, n_second // 2), n_second // 2)
        return x * 2 + lax.rem(lax.rem(sec, 2) + 1 - lax.rem(k, 2), 2)

    barrier = pltpu.get_barrier_semaphore()

    @pl.loop(0, n_hist - 1)
    def _(k):
        pl.semaphore_signal(barrier, 1, device_id=(hist_peer(k), sec), device_id_type=MESH)

    @pl.loop(0, n_second - 1)
    def _(k):
        pl.semaphore_signal(barrier, 1, device_id=(h, second_peer(k)), device_id_type=MESH)

    loads = [
        pltpu.make_async_copy(src, dst, in_sem.at[i])
        for i, (src, dst) in enumerate(
            (
                (start_hbm, start_ref),
                (time_hbm, time_ref),
                (coup_hbm, coup_ref),
                (row_hbm, row_ref),
                (hist_hbm, stored),
                (inv_hbm, inv_ref),
            )
        )
    ]
    for load in loads:
        load.start()
    for load in loads[:4]:
        load.wait()

    anchor = start_ref[0].astype(F32)
    row8 = lax.broadcasted_iota(jnp.int32, (8, times), 0)
    tile = jnp.full((8, times), -1.0, F32)
    for s in range(slots):
        tile = jnp.where(lax.rem(row8, slots) == s, time_ref[s].astype(F32), tile)
    vbuf[h] = tile

    weight_sq = coup_ref[...] * coup_ref[...]

    def put_energy(w, green):
        for b in range(own):
            less, more = green[b][0], green[b][1]
            lr, li, mr, mi = less[:, :half], less[:, half:], more[:, :half], more[:, half:]
            less_r, less_i = cubic_term(lr, li, mr, mi)
            more_r, more_i = cubic_term(mr, mi, lr, li)
            weight = weight_sq[b : b + 1, :]
            both = jnp.concatenate([weight * (more_r - less_r), weight * (more_i - less_i)], axis=1)
            ebuf[w, pl.ds(pl.multiple_of(sec * slab, slab), slab), b * pair : (b + 1) * pair] = both.astype(BF16)

    def send_energy(w):
        mine = ebuf.at[w, pl.ds(pl.multiple_of(sec * slab, slab), slab)]

        @pl.loop(0, n_second - 1)
        def _(k):
            pltpu.make_async_remote_copy(
                mine, mine, a_send.at[w], a_recv.at[w], device_id=(h, second_peer(k)), device_id_type=MESH
            ).start()

    group = n_z * own
    part = 2 * slab * group
    green = [[row_ref[b, :, m * pair : (m + 1) * pair] for m in range(2)] for b in range(own)]
    put_energy(0, green)

    pl.semaphore_wait(barrier, n_second - 1 + n_hist - 1)

    @pl.loop(0, n_hist - 1)
    def _(k):
        pltpu.make_async_remote_copy(
            vbuf.at[h], vbuf.at[h], v_send, v_recv, device_id=(hist_peer(k), sec), device_id_type=MESH
        ).start()

    send_energy(0)

    wide = 2 * slab
    loads[4].wait()

    @pl.loop(0, half)
    def _(j):
        for s in range(slots):
            at = pl.multiple_of((j * slots + s) * wide, wide)
            spread[pl.ds(at, wide), :] = stored[pl.ds(pl.multiple_of((s * half + j) * wide, wide), wide), :].astype(F32)

    index = lax.broadcasted_iota(jnp.int32, (pair, pair), 0)
    place = lax.rem(index // own, n_z)
    depth = jnp.zeros_like(index)
    for n in range(n_z):
        depth = jnp.where(place == n, lax.rem(z + order[n], n_z), depth)
    to_y = lax.rem(lax.rem(index // (own * n_z), n_y) + y, n_y)
    column = ((depth * n_y + to_y) * own + lax.rem(index, own)) * 2 + index // half
    turn = jnp.where(lax.broadcasted_iota(jnp.int32, (pair, pair), 1) == column, 1.0, 0.0).astype(BF16)
    depth_of = half * slots

    @pl.loop(0, slab)
    def _(t):
        for m in range(2):
            block = spread[pl.ds(t * 2 + m, depth_of, stride=wide), :].astype(BF16)
            columns = lax.dot_general(turn, block, (((1,), (1,)), ((), ())), preferred_element_type=F32).astype(BF16)
            for p in range(2):
                for off in range(n_y):
                    at = p * half + off * group
                    turned_hist[
                        off,
                        pl.ds(pl.multiple_of((m * slab + t) * group, group), group),
                        p * depth_of : (p + 1) * depth_of,
                    ] = columns[at : at + group]

    for off in sorted(range(1, n_y), key=lambda o: -min(o, n_y - o)):
        pltpu.make_async_remote_copy(
            turned_hist.at[off],
            held.at[y],
            h_send,
            h_recv,
            device_id=(z * n_y + lax.rem(y + off, n_y), sec),
            device_id_type=MESH,
        ).start()
    held[y] = turned_hist[0]

    wait_bytes(vbuf.at[0 : n_hist - 1], v_recv)
    asked = vbuf[...].reshape(n_hist * 8, times)
    lane = lax.broadcasted_iota(jnp.int32, (n_hist * 8, times), 1).astype(F32)
    onehot[0 : n_hist * 8, :] = jnp.where((asked == lane) & (asked <= anchor), 1.0, 0.0).astype(BF16)
    row16 = lax.broadcasted_iota(jnp.int32, (16, times), 0)
    lane16 = lax.broadcasted_iota(jnp.int32, (16, times), 1).astype(F32)
    later = anchor + 1.0 + lax.rem(row16, 2).astype(F32)
    onehot[n_hist * 8 : n_hist * 8 + 16, :] = jnp.where((later == lane16) & (row16 < 2 * own), 1.0, 0.0).astype(BF16)

    loads[5].wait()
    past = []
    for w in range(steps):
        wait_bytes(ebuf.at[w, 0 : times - slab], a_recv.at[w])
        picked = jnp.dot(onehot[...], ebuf[w], preferred_element_type=F32)
        sub = lax.rem(lax.broadcasted_iota(jnp.int32, (n_hist * 8, pair), 0), 8)
        chosen = jnp.where(sub < slots, picked[: n_hist * 8, :pair], picked[: n_hist * 8, pair:])
        sendb[w] = chosen.reshape(n_z, n_y * 8, pair).astype(BF16)
        if w:
            extra = picked[n_hist * 8 : n_hist * 8 + 16]
            sub16 = lax.broadcasted_iota(jnp.int32, (16, pair), 0)
            sendx[w] = jnp.where(sub16 < 2, extra[:, :pair], extra[:, pair:]).astype(BF16)

        @pl.loop(0, n_hist - 1)
        def _(k, w=w):
            to = hist_peer(k)
            pltpu.make_async_remote_copy(
                sendb.at[w, to // n_y],
                recvb.at[w, h],
                b_send.at[w],
                b_recv.at[w],
                device_id=(to, sec),
                device_id_type=MESH,
            ).start()

        recvb[w, h] = sendb[w, z]
        if w:

            @pl.loop(0, n_hist - 1)
            def _(k, w=w):
                pltpu.make_async_remote_copy(
                    sendx.at[w],
                    recvx.at[w, h],
                    x_send.at[w],
                    x_recv.at[w],
                    device_id=(hist_peer(k), sec),
                    device_id_type=MESH,
                ).start()

            recvx[w, h] = sendx[w]
        wait_bytes(recvb.at[w, 0 : n_hist - 1], b_recv.at[w])
        got = recvb[w].astype(F32)
        if w == 0:
            wait_bytes(held.at[0 : n_y - 1], h_recv)

        product = None
        for k in range(n_y):
            left = got[:, k * 8 : (k + 1) * 8].reshape(n_hist * 8, pair)
            weights = jnp.concatenate([left, turned(left, half)], axis=0).astype(BF16)
            term = jnp.dot(held[k], weights, preferred_element_type=F32)
            product = term if product is None else product + term
        summed[...] = product
        total = None
        for n in range(n_z):
            piece = jnp.concatenate(
                [summed[pl.ds(n * own + b, 2 * slab, stride=group), :] for b in range(own)], axis=0
            )
            if order[n] == 0:
                total = piece
                continue
            sendz[w, n] = piece.astype(BF16)
            pltpu.make_async_remote_copy(
                sendz.at[w, n],
                recvz.at[w, n],
                z_send.at[w],
                z_recv.at[w],
                device_id=(lax.rem(z + order[n], n_z) * n_y + y, sec),
                device_id_type=MESH,
            ).start()

        local = [[green[b][m] for m in range(2)] for b in range(own)]
        recent = None
        if w:
            wait_bytes(recvx.at[w, 0 : n_hist - 1], x_recv.at[w])
            tail = recvx[w].reshape(n_hist * 16, pair)
            rec = [None] * w
            for i in range(w):
                orbital = lax.broadcasted_iota(jnp.int32, (half, n_hist * 16), 0)
                at = lax.broadcasted_iota(jnp.int32, (half, n_hist * 16), 1)
                pick = jnp.where(at == (orbital // own) * 16 + lax.rem(orbital, own) * 2 + i, 1.0, 0.0).astype(BF16)
                column = jnp.dot(pick, tail, preferred_element_type=F32)
                matrix = jnp.concatenate([column, turned(column, half)], axis=0)
                rec[i] = jnp.dot(past[i], matrix, precision=HIGHEST, preferred_element_type=F32)
            recent = rec[0] if w == 1 else rec[0] + rec[1]

        wait_bytes(recvz.at[w], z_recv.at[w])
        for n in range(n_z - 1):
            total = total + recvz[w, n].astype(F32)
        if recent is not None:
            total = total + recent

        current = jnp.concatenate([local[b][m] for b in range(own) for m in range(2)], axis=0)
        moved = current + STEP_WIDTH * total
        real, imag = inv_ref[w, 0], inv_ref[w, 1]
        advance = jnp.concatenate(
            [jnp.concatenate([real, -imag], axis=1), jnp.concatenate([imag, real], axis=1)], axis=0
        )
        new = lax.dot_general(
            moved, advance, (((1,), (1,)), ((), ())), precision=HIGHEST, preferred_element_type=F32
        )
        past.append(new)
        split = new.reshape(own, 2, slab, pair)
        green = [[split[b, m] for m in range(2)] for b in range(own)]
        if w + 1 < steps:
            put_energy(w + 1, green)
            send_energy(w + 1)
        else:
            for b in range(own):
                for m in range(2):
                    out_ref[b, :, m * pair : (m + 1) * pair] = green[b][m]

    wait_bytes(vbuf.at[0 : n_hist - 1], v_send)
    wait_bytes(held.at[0 : n_y - 1], h_send)
    for w in range(steps):
        wait_bytes(ebuf.at[w, 0 : times - slab], a_send.at[w])
        wait_bytes(recvb.at[w, 0 : n_hist - 1], b_send.at[w])
        if w:
            wait_bytes(recvx.at[w, 0 : n_hist - 1], x_send.at[w])
        wait_bytes(recvz.at[w], z_send.at[w])


def body(n_hist, n_second, n_y, history, row_now, coupling, step_inverse, start_step, history_time):
    slots, orbitals, slab = history.shape[:3]
    own = row_now.shape[0]
    pair = 2 * orbitals
    n_z = n_hist // n_y
    steps = step_inverse.shape[0]
    times = slab * n_second
    rows = own * 2 * slab
    order = sorted(range(n_z), key=lambda d: (-min(d, n_z - d), d))
    dims = (n_hist, n_second, n_y, tuple(order), steps)
    part = rows * n_z
    blocks = history.reshape(slots * orbitals * slab * 2, pair)
    vmem = pl.BlockSpec(memory_space=pltpu.VMEM)
    dma = pltpu.SemaphoreType.DMA
    return pl.pallas_call(
        functools.partial(kernel, dims),
        out_shape=jax.ShapeDtypeStruct(row_now.shape, F32),
        in_specs=[pl.BlockSpec(memory_space=pltpu.HBM)] * 6,
        out_specs=vmem,
        scratch_shapes=[
            pltpu.VMEM(row_now.shape, F32),
            pltpu.VMEM(coupling.shape, F32),
            pltpu.VMEM(step_inverse.shape, F32),
            pltpu.SMEM(start_step.shape, jnp.int32),
            pltpu.SMEM(history_time.shape, jnp.int32),
            pltpu.VMEM(blocks.shape, BF16),
            pltpu.VMEM(blocks.shape, F32),
            pltpu.VMEM((n_y, part, pair * slots), BF16),
            pltpu.VMEM((n_y, part, pair * slots), BF16),
            pltpu.VMEM((steps, times, own * pair), BF16),
            pltpu.VMEM((n_hist, 8, times), F32),
            pltpu.VMEM((n_hist * 8 + 16, times), BF16),
            pltpu.VMEM((steps, n_z, n_y * 8, pair), BF16),
            pltpu.VMEM((steps, n_hist, n_y * 8, pair), BF16),
            pltpu.VMEM((steps, 16, pair), BF16),
            pltpu.VMEM((steps, n_hist, 16, pair), BF16),
            pltpu.VMEM((part, pair), F32),
            pltpu.VMEM((steps, n_z - 1, rows, pair), BF16),
            pltpu.VMEM((steps, n_z - 1, rows, pair), BF16),
            dma((6,)),
            dma,
            dma,
            dma((steps,)),
            dma((steps,)),
            dma((steps,)),
            dma((steps,)),
            dma((steps,)),
            dma((steps,)),
            dma,
            dma,
            dma((steps,)),
            dma((steps,)),
        ],
        compiler_params=pltpu.CompilerParams(
            collective_id=0, has_side_effects=True, vmem_limit_bytes=63 * 1024 * 1024
        ),
    )(blocks, row_now, coupling, step_inverse, start_step, history_time)


def solution(mesh):
    placed = (
        P("hist", None, "second", None, None),
        P("hist", "second", None),
        P("hist", None),
        P(),
        P(),
        P("hist"),
    )
    return jax.shard_map(
        functools.partial(body, mesh.shape["hist"], mesh.shape["second"], CHIPS_Y),
        mesh=mesh,
        in_specs=placed,
        out_specs=P("hist", "second", None),
        check_vma=False,
    )
```

```python
import functools

import jax
import jax.numpy as jnp
from jax import lax
from jax.experimental import pallas as pl
from jax.experimental.pallas import tpu as pltpu
from jax.sharding import PartitionSpec as P

MESH = pl.DeviceIdType.MESH
HIGHEST = lax.Precision.HIGHEST
STEP_WIDTH = 0.05
CHIPS_Y = 4
F32 = jnp.float32
BF16 = jnp.bfloat16


def cubic_term(first_real, first_imag, other_real, other_imag):
    square_real = first_real * first_real - first_imag * first_imag
    square_imag = 2.0 * first_real * first_imag
    return (
        square_real * other_real + square_imag * other_imag,
        square_imag * other_real - square_real * other_imag,
    )


def turned(pair, half):
    return jnp.concatenate([-pair[:, half:], pair[:, :half]], axis=1)


def wait_bytes(ref, sem):
    pltpu.make_async_copy(ref, ref, sem).wait()


def kernel(
    dims,
    hist_hbm,
    row_hbm,
    coup_hbm,
    inv_hbm,
    start_hbm,
    time_hbm,
    out_ref,
    row_ref,
    coup_ref,
    inv_ref,
    start_ref,
    time_ref,
    stored,
    spread,
    h2,
    ebuf,
    vbuf,
    onehot,
    sendb,
    recvb,
    sendy,
    recvy,
    zown,
    summed,
    sendz,
    recvz,
    in_sem,
    v_send,
    v_recv,
    a_send,
    a_recv,
    b_send,
    b_recv,
    y_send,
    y_recv,
    z_send,
    z_recv,
):
    n_hist, n_second, n_y, order, cuts, steps = dims
    n_z = n_hist // n_y
    own, slab, width = row_ref.shape
    half = width // 4
    pair = 2 * half
    slots = time_ref.shape[0]
    times = ebuf.shape[1]
    rows = own * 2 * slab
    h = lax.axis_index("hist")
    sec = lax.axis_index("second")
    z = h // n_y
    y = lax.rem(h, n_y)

    def outward(k, n):
        step = (k + 1) // 2
        return n // 2 + step - 2 * step * lax.rem(k, 2)

    def hist_peer(k):
        return lax.rem(z + outward(k // n_y, n_z), n_z) * n_y + lax.rem(y + outward(lax.rem(k, n_y), n_y), n_y)

    def second_peer(k):
        x = lax.rem(sec // 2 + outward(k // 2, n_second // 2), n_second // 2)
        return x * 2 + lax.rem(lax.rem(sec, 2) + 1 - lax.rem(k, 2), 2)

    barrier = pltpu.get_barrier_semaphore()

    @pl.loop(0, n_hist - 1)
    def _(k):
        pl.semaphore_signal(barrier, 1, device_id=(hist_peer(k), sec), device_id_type=MESH)

    @pl.loop(0, n_second - 1)
    def _(k):
        pl.semaphore_signal(barrier, 1, device_id=(h, second_peer(k)), device_id_type=MESH)

    loads = [
        pltpu.make_async_copy(src, dst, in_sem.at[i])
        for i, (src, dst) in enumerate(
            (
                (start_hbm, start_ref),
                (time_hbm, time_ref),
                (coup_hbm, coup_ref),
                (row_hbm, row_ref),
                (hist_hbm, stored),
                (inv_hbm, inv_ref),
            )
        )
    ]
    for load in loads:
        load.start()
    for load in loads[:4]:
        load.wait()

    anchor = start_ref[0].astype(F32)
    row8 = lax.broadcasted_iota(jnp.int32, (8, times), 0)
    tile = jnp.full((8, times), -1.0, F32)
    for s in range(slots):
        held = time_ref[s].astype(F32)
        tile = jnp.where(lax.rem(row8, slots) == s, held, tile)
    vbuf[h] = tile

    weight_sq = coup_ref[...] * coup_ref[...]

    def put_energy(w, green):
        for b in range(own):
            less, more = green[b][0], green[b][1]
            lr, li, mr, mi = less[:, :half], less[:, half:], more[:, :half], more[:, half:]
            less_r, less_i = cubic_term(lr, li, mr, mi)
            more_r, more_i = cubic_term(mr, mi, lr, li)
            weight = weight_sq[b : b + 1, :]
            both = jnp.concatenate([weight * (more_r - less_r), weight * (more_i - less_i)], axis=1)
            ebuf[w, pl.ds(pl.multiple_of(sec * slab, slab), slab), b * pair : (b + 1) * pair] = both.astype(BF16)

    def send_energy(w):
        mine = ebuf.at[w, pl.ds(pl.multiple_of(sec * slab, slab), slab)]

        @pl.loop(0, n_second - 1)
        def _(k):
            pltpu.make_async_remote_copy(
                mine, mine, a_send.at[w], a_recv.at[w], device_id=(h, second_peer(k)), device_id_type=MESH
            ).start()

    part = 2 * slab * (n_z // len(cuts)) * own
    green = [[row_ref[b, :, m * pair : (m + 1) * pair] for m in range(2)] for b in range(own)]
    put_energy(0, green)

    wide = 2 * slab
    loads[4].wait()

    @pl.loop(0, half)
    def _(j):
        for s in range(slots):
            at = pl.multiple_of((j * slots + s) * wide, wide)
            spread[pl.ds(at, wide), :] = stored[pl.ds(pl.multiple_of((s * half + j) * wide, wide), wide), :].astype(F32)

    pl.semaphore_wait(barrier, n_second - 1 + n_hist - 1)

    @pl.loop(0, n_hist - 1)
    def _(k):
        pltpu.make_async_remote_copy(
            vbuf.at[h], vbuf.at[h], v_send, v_recv, device_id=(hist_peer(k), sec), device_id_type=MESH
        ).start()

    send_energy(0)

    index = lax.broadcasted_iota(jnp.int32, (pair, pair), 0)
    place = lax.rem(index // own, n_z)
    depth = jnp.zeros_like(index)
    for n in range(n_z):
        depth = jnp.where(place == n, lax.rem(z + order[n], n_z), depth)
    to_y = lax.rem(lax.rem(index // (own * n_z), n_y) + y, n_y)
    column = ((depth * n_y + to_y) * own + lax.rem(index, own)) * 2 + index // half
    turn = jnp.where(lax.broadcasted_iota(jnp.int32, (pair, pair), 1) == column, 1.0, 0.0).astype(BF16)
    depth_of = half * slots
    unit = (n_z // len(cuts)) * own

    @pl.loop(0, slab // 2)
    def _(u):
        for m in range(2):
            both = []
            for k in range(2):
                block = spread[pl.ds((2 * u + k) * 2 + m, depth_of, stride=wide), :].astype(BF16)
                both.append(
                    lax.dot_general(turn, block, (((1,), (1,)), ((), ())), preferred_element_type=F32)
                )
            for p in range(2):
                for off in range(n_y):
                    for c in range(len(cuts)):
                        at = p * half + (off * len(cuts) + c) * unit
                        h2[
                            c,
                            off,
                            pl.ds(pl.multiple_of((m * slab + 2 * u) * unit, 2 * unit), 2 * unit),
                            p * depth_of : (p + 1) * depth_of,
                        ] = jnp.concatenate([one[at : at + unit] for one in both], axis=0).astype(BF16)

    wait_bytes(vbuf.at[0 : n_hist - 1], v_recv)
    asked = vbuf[...].reshape(n_hist * 8, times)
    lane = lax.broadcasted_iota(jnp.int32, (n_hist * 8, times), 1).astype(F32)
    onehot[0 : n_hist * 8, :] = jnp.where((asked == lane) & (asked <= anchor), 1.0, 0.0).astype(BF16)
    row16 = lax.broadcasted_iota(jnp.int32, (16, times), 0)
    lane16 = lax.broadcasted_iota(jnp.int32, (16, times), 1).astype(F32)
    later = anchor + 1.0 + lax.rem(row16, 2).astype(F32)
    onehot[n_hist * 8 : n_hist * 8 + 16, :] = jnp.where((later == lane16) & (row16 < 2 * own), 1.0, 0.0).astype(BF16)

    loads[5].wait()
    past = []
    for w in range(steps):
        wait_bytes(ebuf.at[w, 0 : times - slab], a_recv.at[w])
        picked = jnp.dot(onehot[...], ebuf[w], preferred_element_type=F32)
        sub = lax.rem(lax.broadcasted_iota(jnp.int32, (n_hist * 8, pair), 0), 8)
        chosen = jnp.where(sub < slots, picked[: n_hist * 8, :pair], picked[: n_hist * 8, pair:])
        sub8 = lax.broadcasted_iota(jnp.int32, (8, pair), 0)
        extra = picked[n_hist * 8 : n_hist * 8 + 8]
        extra = jnp.where(sub8 < 2, extra[:, :pair], extra[:, pair:])
        piece = jnp.concatenate(
            [chosen.reshape(n_hist, 8, pair), jnp.broadcast_to(extra[None], (n_hist, 8, pair))], axis=1
        )
        sendb[w] = piece.astype(BF16)

        @pl.loop(0, n_hist - 1)
        def _(k, w=w):
            to = hist_peer(k)
            pltpu.make_async_remote_copy(
                sendb.at[w, to], recvb.at[w, h], b_send.at[w], b_recv.at[w], device_id=(to, sec), device_id_type=MESH
            ).start()

        recvb[w, h] = sendb[w, h]
        wait_bytes(recvb.at[w, 0 : n_hist - 1], b_recv.at[w])
        got = recvb[w].astype(F32)
        left = got[:, :8].reshape(n_hist * 8, pair)
        weights = jnp.concatenate([left, turned(left, half)], axis=0).astype(BF16)

        for c in range(len(cuts)):
            product = jnp.dot(
                h2[c, 1:].reshape((n_y - 1) * part, pair * slots), weights, preferred_element_type=F32
            ).astype(BF16)
            for off in range(1, n_y):
                sendy[w, c, off - 1] = product[(off - 1) * part : off * part]
            for m in range(2):
                for off in sorted(range(1, n_y), key=lambda o: -min(o, n_y - o)):
                    own_m = (w, c, off - 1, pl.ds(m * part // 2, part // 2))
                    pltpu.make_async_remote_copy(
                        sendy.at[own_m],
                        recvy.at[own_m],
                        y_send.at[w],
                        y_recv.at[w, c, m],
                        device_id=(z * n_y + lax.rem(y + off, n_y), sec),
                        device_id_type=MESH,
                    ).start()
        for c in range(len(cuts)):
            zown[c] = jnp.dot(h2[c, 0], weights, preferred_element_type=F32)

        local = [[green[b][m] for m in range(2)] for b in range(own)]
        recent = None
        if w:
            tail = got[:, 8:].reshape(n_hist * 8, pair).astype(BF16)
            rec = [None] * w
            for i in range(w):
                orbital = lax.broadcasted_iota(jnp.int32, (half, n_hist * 8), 0)
                at = lax.broadcasted_iota(jnp.int32, (half, n_hist * 8), 1)
                pick = jnp.where(at == (orbital // own) * 8 + lax.rem(orbital, own) * 2 + i, 1.0, 0.0).astype(BF16)
                column = jnp.dot(pick, tail, preferred_element_type=F32)
                matrix = jnp.concatenate([column, turned(column, half)], axis=0)
                rec[i] = jnp.dot(past[i], matrix, precision=HIGHEST, preferred_element_type=F32)
            recent = rec[0] if w == 1 else rec[0] + rec[1]

        totals = [None, None]
        for c, (first, last) in enumerate(cuts):
            for m in range(2):
                of_m = pl.ds(m * part // 2, part // 2)
                wait_bytes(recvy.at[w, c, :, of_m], y_recv.at[w, c, m])
                acc = zown[c, of_m]
                for k in range(n_y - 1):
                    acc = acc + recvy[w, c, k, of_m].astype(F32)
                summed[c, of_m] = acc
                for n in range(first, last):
                    piece = jnp.concatenate(
                        [
                            summed[c, pl.ds(m * part // 2 + (n - first) * own + b, slab, stride=unit), :]
                            for b in range(own)
                        ],
                        axis=0,
                    )
                    if order[n] == 0:
                        totals[m] = piece
                        continue
                    sendz[w, n, m] = piece.astype(BF16)
                    pltpu.make_async_remote_copy(
                        sendz.at[w, n, m],
                        recvz.at[w, n, m],
                        z_send.at[w],
                        z_recv.at[w],
                        device_id=(lax.rem(z + order[n], n_z) * n_y + y, sec),
                        device_id_type=MESH,
                    ).start()
        wait_bytes(recvz.at[w], z_recv.at[w])
        for n in range(n_z - 1):
            totals = [totals[m] + recvz[w, n, m].astype(F32) for m in range(2)]
        total = jnp.concatenate(totals, axis=0)
        if recent is not None:
            total = total + recent

        current = jnp.concatenate([local[b][m] for m in range(2) for b in range(own)], axis=0)
        moved = current + STEP_WIDTH * total
        real, imag = inv_ref[w, 0], inv_ref[w, 1]
        advance = jnp.concatenate(
            [jnp.concatenate([real, -imag], axis=1), jnp.concatenate([imag, real], axis=1)], axis=0
        )
        new = lax.dot_general(
            moved, advance, (((1,), (1,)), ((), ())), precision=HIGHEST, preferred_element_type=F32
        )
        past.append(new)
        split = new.reshape(2, own, slab, pair)
        green = [[split[m, b] for m in range(2)] for b in range(own)]
        if w + 1 < steps:
            put_energy(w + 1, green)
            send_energy(w + 1)
        else:
            for b in range(own):
                for m in range(2):
                    out_ref[b, :, m * pair : (m + 1) * pair] = green[b][m]

    wait_bytes(vbuf.at[0 : n_hist - 1], v_send)
    for w in range(steps):
        wait_bytes(ebuf.at[w, 0 : times - slab], a_send.at[w])
        wait_bytes(recvb.at[w, 0 : n_hist - 1], b_send.at[w])
        wait_bytes(recvy.at[w], y_send.at[w])
        wait_bytes(recvz.at[w], z_send.at[w])


def body(n_hist, n_second, n_y, history, row_now, coupling, step_inverse, start_step, history_time):
    slots, orbitals, slab = history.shape[:3]
    own = row_now.shape[0]
    pair = 2 * orbitals
    n_z = n_hist // n_y
    steps = step_inverse.shape[0]
    times = slab * n_second
    rows = own * 2 * slab
    order = sorted(range(n_z), key=lambda d: (-min(d, n_z - d), d))
    cuts = ((0, n_z // 2), (n_z // 2, n_z))
    dims = (n_hist, n_second, n_y, tuple(order), cuts, steps)
    part = rows * n_z // len(cuts)
    blocks = history.reshape(slots * orbitals * slab * 2, pair)
    vmem = pl.BlockSpec(memory_space=pltpu.VMEM)
    dma = pltpu.SemaphoreType.DMA
    return pl.pallas_call(
        functools.partial(kernel, dims),
        out_shape=jax.ShapeDtypeStruct(row_now.shape, F32),
        in_specs=[pl.BlockSpec(memory_space=pltpu.HBM)] * 6,
        out_specs=vmem,
        scratch_shapes=[
            pltpu.VMEM(row_now.shape, F32),
            pltpu.VMEM(coupling.shape, F32),
            pltpu.VMEM(step_inverse.shape, F32),
            pltpu.SMEM(start_step.shape, jnp.int32),
            pltpu.SMEM(history_time.shape, jnp.int32),
            pltpu.VMEM(blocks.shape, BF16),
            pltpu.VMEM(blocks.shape, F32),
            pltpu.VMEM((len(cuts), n_y, part, pair * slots), BF16),
            pltpu.VMEM((steps, times, own * pair), BF16),
            pltpu.VMEM((n_hist, 8, times), F32),
            pltpu.VMEM((n_hist * 8 + 16, times), BF16),
            pltpu.VMEM((steps, n_hist, 16, pair), BF16),
            pltpu.VMEM((steps, n_hist, 16, pair), BF16),
            pltpu.VMEM((steps, len(cuts), n_y - 1, part, pair), BF16),
            pltpu.VMEM((steps, len(cuts), n_y - 1, part, pair), BF16),
            pltpu.VMEM((len(cuts), part, pair), F32),
            pltpu.VMEM((len(cuts), part, pair), F32),
            pltpu.VMEM((steps, n_z - 1, 2, own * slab, pair), BF16),
            pltpu.VMEM((steps, n_z - 1, 2, own * slab, pair), BF16),
            dma((6,)),
            dma,
            dma,
            dma((steps,)),
            dma((steps,)),
            dma((steps,)),
            dma((steps,)),
            dma((steps,)),
            dma((steps, len(cuts), 2)),
            dma((steps,)),
            dma((steps,)),
        ],
        compiler_params=pltpu.CompilerParams(
            collective_id=0, has_side_effects=True, vmem_limit_bytes=63 * 1024 * 1024
        ),
    )(blocks, row_now, coupling, step_inverse, start_step, history_time)


def solution(mesh):
    placed = (
        P("hist", None, "second", None, None),
        P("hist", "second", None),
        P("hist", None),
        P(),
        P(),
        P("hist"),
    )
    return jax.shard_map(
        functools.partial(body, mesh.shape["hist"], mesh.shape["second"], CHIPS_Y),
        mesh=mesh,
        in_specs=placed,
        out_specs=P("hist", "second", None),
        check_vma=False,
    )
```

```python
import functools

import jax
import jax.numpy as jnp
from jax import lax
from jax.experimental import pallas as pl
from jax.experimental.pallas import tpu as pltpu
from jax.sharding import PartitionSpec as P

MESH = pl.DeviceIdType.MESH
HIGHEST = lax.Precision.HIGHEST
STEP_WIDTH = 0.05
CHIPS_Y = 4
F32 = jnp.float32
BF16 = jnp.bfloat16


def cubic_term(first_real, first_imag, other_real, other_imag):
    square_real = first_real * first_real - first_imag * first_imag
    square_imag = 2.0 * first_real * first_imag
    return (
        square_real * other_real + square_imag * other_imag,
        square_imag * other_real - square_real * other_imag,
    )


def turned(pair, half):
    return jnp.concatenate([-pair[:, half:], pair[:, :half]], axis=1)


def wait_bytes(ref, sem):
    pltpu.make_async_copy(ref, ref, sem).wait()


def kernel(
    dims,
    hist_hbm,
    row_hbm,
    coup_hbm,
    inv_hbm,
    start_hbm,
    time_hbm,
    out_ref,
    row_ref,
    coup_ref,
    inv_ref,
    start_ref,
    time_ref,
    stored,
    spread,
    h2,
    ebuf,
    vbuf,
    onehot,
    sendb,
    recvb,
    sendy,
    recvy,
    zown,
    summed,
    sendz,
    recvz,
    in_sem,
    v_send,
    v_recv,
    a_send,
    a_recv,
    b_send,
    b_recv,
    y_send,
    y_recv,
    z_send,
    z_recv,
):
    n_hist, n_second, n_y, order, cuts, steps = dims
    n_z = n_hist // n_y
    own, slab, width = row_ref.shape
    half = width // 4
    pair = 2 * half
    slots = time_ref.shape[0]
    times = ebuf.shape[1]
    rows = own * 2 * slab
    h = lax.axis_index("hist")
    sec = lax.axis_index("second")
    z = h // n_y
    y = lax.rem(h, n_y)

    def outward(k, n):
        step = (k + 1) // 2
        return n // 2 + step - 2 * step * lax.rem(k, 2)

    def second_peer(k):
        x = lax.rem(sec // 2 + outward(k // 2, n_second // 2), n_second // 2)
        return x * 2 + lax.rem(lax.rem(sec, 2) + 1 - lax.rem(k, 2), 2)

    far_first = sorted(((dz, dy) for dz in range(n_z) for dy in range(n_y) if dz or dy), key=lambda d: -min(d[0], n_z - d[0]) - min(d[1], n_y - d[1]))

    barrier = pltpu.get_barrier_semaphore()

    for dz, dy in far_first:
        to = lax.rem(z + dz, n_z) * n_y + lax.rem(y + dy, n_y)
        pl.semaphore_signal(barrier, 1, device_id=(to, sec), device_id_type=MESH)

    @pl.loop(0, n_second - 1)
    def _(k):
        pl.semaphore_signal(barrier, 1, device_id=(h, second_peer(k)), device_id_type=MESH)

    loads = [
        pltpu.make_async_copy(src, dst, in_sem.at[i])
        for i, (src, dst) in enumerate(
            (
                (start_hbm, start_ref),
                (time_hbm, time_ref),
                (coup_hbm, coup_ref),
                (row_hbm, row_ref),
                (hist_hbm, stored),
                (inv_hbm, inv_ref),
            )
        )
    ]
    for load in loads:
        load.start()
    for load in loads[:4]:
        load.wait()

    anchor = start_ref[0].astype(F32)
    row8 = lax.broadcasted_iota(jnp.int32, (8, times), 0)
    tile = jnp.full((8, times), -1.0, F32)
    for s in range(slots):
        held = time_ref[s].astype(F32)
        tile = jnp.where(lax.rem(row8, slots) == s, held, tile)
    vbuf[h] = tile

    weight_sq = coup_ref[...] * coup_ref[...]

    def put_energy(w, green):
        for b in range(own):
            less, more = green[b][0], green[b][1]
            lr, li, mr, mi = less[:, :half], less[:, half:], more[:, :half], more[:, half:]
            less_r, less_i = cubic_term(lr, li, mr, mi)
            more_r, more_i = cubic_term(mr, mi, lr, li)
            weight = weight_sq[b : b + 1, :]
            both = jnp.concatenate([weight * (more_r - less_r), weight * (more_i - less_i)], axis=1)
            ebuf[w, pl.ds(pl.multiple_of(sec * slab, slab), slab), b * pair : (b + 1) * pair] = both.astype(BF16)

    def send_energy(w):
        mine = ebuf.at[w, pl.ds(pl.multiple_of(sec * slab, slab), slab)]

        @pl.loop(0, n_second - 1)
        def _(k):
            pltpu.make_async_remote_copy(
                mine, mine, a_send.at[w], a_recv.at[w], device_id=(h, second_peer(k)), device_id_type=MESH
            ).start()

    part = 2 * slab * (n_z // len(cuts)) * own
    green = [[row_ref[b, :, m * pair : (m + 1) * pair] for m in range(2)] for b in range(own)]
    put_energy(0, green)

    wide = 2 * slab
    loads[4].wait()

    @pl.loop(0, half)
    def _(j):
        for s in range(slots):
            at = pl.multiple_of((j * slots + s) * wide, wide)
            spread[pl.ds(at, wide), :] = stored[pl.ds(pl.multiple_of((s * half + j) * wide, wide), wide), :].astype(F32)

    pl.semaphore_wait(barrier, n_second - 1 + n_hist - 1)

    for dz, dy in far_first:
        to = lax.rem(z + dz, n_z) * n_y + lax.rem(y + dy, n_y)
        pltpu.make_async_remote_copy(
            vbuf.at[h], vbuf.at[h], v_send, v_recv, device_id=(to, sec), device_id_type=MESH
        ).start()

    send_energy(0)

    index = lax.broadcasted_iota(jnp.int32, (pair, pair), 0)
    place = lax.rem(index // own, n_z)
    depth = jnp.zeros_like(index)
    for n in range(n_z):
        depth = jnp.where(place == n, lax.rem(z + order[n], n_z), depth)
    to_y = lax.rem(lax.rem(index // (own * n_z), n_y) + y, n_y)
    column = ((depth * n_y + to_y) * own + lax.rem(index, own)) * 2 + index // half
    turn = jnp.where(lax.broadcasted_iota(jnp.int32, (pair, pair), 1) == column, 1.0, 0.0).astype(BF16)
    depth_of = half * slots
    unit = (n_z // len(cuts)) * own

    @pl.loop(0, slab // 2)
    def _(u):
        for m in range(2):
            both = []
            for k in range(2):
                block = spread[pl.ds((2 * u + k) * 2 + m, depth_of, stride=wide), :].astype(BF16)
                both.append(
                    lax.dot_general(turn, block, (((1,), (1,)), ((), ())), preferred_element_type=F32)
                )
            for p in range(2):
                for off in range(n_y):
                    for c in range(len(cuts)):
                        at = p * half + (off * len(cuts) + c) * unit
                        h2[
                            c,
                            off,
                            pl.ds(pl.multiple_of((m * slab + 2 * u) * unit, 2 * unit), 2 * unit),
                            p * depth_of : (p + 1) * depth_of,
                        ] = jnp.concatenate([one[at : at + unit] for one in both], axis=0).astype(BF16)

    wait_bytes(vbuf.at[0 : n_hist - 1], v_recv)
    asked = vbuf[...].reshape(n_hist * 8, times)
    lane = lax.broadcasted_iota(jnp.int32, (n_hist * 8, times), 1).astype(F32)
    onehot[0 : n_hist * 8, :] = jnp.where((asked == lane) & (asked <= anchor), 1.0, 0.0).astype(BF16)
    row16 = lax.broadcasted_iota(jnp.int32, (16, times), 0)
    lane16 = lax.broadcasted_iota(jnp.int32, (16, times), 1).astype(F32)
    later = anchor + 1.0 + lax.rem(row16, 2).astype(F32)
    onehot[n_hist * 8 : n_hist * 8 + 16, :] = jnp.where((later == lane16) & (row16 < 2 * own), 1.0, 0.0).astype(BF16)

    loads[5].wait()
    past = []
    for w in range(steps):
        wait_bytes(ebuf.at[w, 0 : times - slab], a_recv.at[w])
        picked = jnp.dot(onehot[...], ebuf[w], preferred_element_type=F32)
        sub = lax.rem(lax.broadcasted_iota(jnp.int32, (n_hist * 8, pair), 0), 8)
        chosen = jnp.where(sub < slots, picked[: n_hist * 8, :pair], picked[: n_hist * 8, pair:])
        sub8 = lax.broadcasted_iota(jnp.int32, (8, pair), 0)
        extra = picked[n_hist * 8 : n_hist * 8 + 8]
        extra = jnp.where(sub8 < 2, extra[:, :pair], extra[:, pair:])
        piece = jnp.concatenate(
            [chosen.reshape(n_hist, 8, pair), jnp.broadcast_to(extra[None], (n_hist, 8, pair))], axis=1
        )
        sendb[w] = piece.astype(BF16)

        for dz, dy in far_first:
            to = lax.rem(z + dz, n_z) * n_y + lax.rem(y + dy, n_y)
            pltpu.make_async_remote_copy(
                sendb.at[w, to], recvb.at[w, h], b_send.at[w], b_recv.at[w], device_id=(to, sec), device_id_type=MESH
            ).start()

        recvb[w, h] = sendb[w, h]
        wait_bytes(recvb.at[w, 0 : n_hist - 1], b_recv.at[w])
        got = recvb[w].astype(F32)
        left = got[:, :8].reshape(n_hist * 8, pair)
        weights = jnp.concatenate([left, turned(left, half)], axis=0).astype(BF16)

        for c in range(len(cuts)):
            def send(off, m, c=c):
                own_m = (w, c, off - 1, pl.ds(m * part // 2, part // 2))
                pltpu.make_async_remote_copy(
                    sendy.at[own_m],
                    recvy.at[own_m],
                    y_send.at[w],
                    y_recv.at[w, c, m],
                    device_id=(z * n_y + lax.rem(y + off, n_y), sec),
                    device_id_type=MESH,
                ).start()

            offs = sorted(range(1, n_y), key=lambda o: -min(o, n_y - o))
            for off in offs:
                sendy[w, c, off - 1] = jnp.dot(h2[c, off], weights, preferred_element_type=F32).astype(BF16)
                send(off, 0)
            for off in offs:
                send(off, 1)
        for c in range(len(cuts)):
            zown[c] = jnp.dot(h2[c, 0], weights, preferred_element_type=F32)

        local = [[green[b][m] for m in range(2)] for b in range(own)]
        recent = None
        if w:
            tail = got[:, 8:].reshape(n_hist * 8, pair).astype(BF16)
            rec = [None] * w
            for i in range(w):
                orbital = lax.broadcasted_iota(jnp.int32, (half, n_hist * 8), 0)
                at = lax.broadcasted_iota(jnp.int32, (half, n_hist * 8), 1)
                pick = jnp.where(at == (orbital // own) * 8 + lax.rem(orbital, own) * 2 + i, 1.0, 0.0).astype(BF16)
                column = jnp.dot(pick, tail, preferred_element_type=F32)
                matrix = jnp.concatenate([column, turned(column, half)], axis=0)
                rec[i] = jnp.dot(past[i], matrix, precision=HIGHEST, preferred_element_type=F32)
            recent = rec[0] if w == 1 else rec[0] + rec[1]

        real, imag = inv_ref[w, 0], inv_ref[w, 1]
        advance = jnp.concatenate(
            [jnp.concatenate([real, -imag], axis=1), jnp.concatenate([imag, real], axis=1)], axis=0
        )
        coarse = advance.astype(BF16)
        advance = jnp.concatenate([coarse, (advance - coarse.astype(F32)).astype(BF16), coarse], axis=1)
        totals = [None, None]
        for c, (first, last) in enumerate(cuts):
            for m in range(2):
                of_m = pl.ds(m * part // 2, part // 2)
                wait_bytes(recvy.at[w, c, :, of_m], y_recv.at[w, c, m])
                acc = zown[c, of_m]
                for k in range(n_y - 1):
                    acc = acc + recvy[w, c, k, of_m].astype(F32)
                summed[c, of_m] = acc
                for n in range(first, last):
                    piece = jnp.concatenate(
                        [
                            summed[c, pl.ds(m * part // 2 + (n - first) * own + b, slab, stride=unit), :]
                            for b in range(own)
                        ],
                        axis=0,
                    )
                    if order[n] == 0:
                        totals[m] = piece
                        continue
                    sendz[w, n, m] = piece.astype(BF16)
                    pltpu.make_async_remote_copy(
                        sendz.at[w, n, m],
                        recvz.at[w, n, m],
                        z_send.at[w],
                        z_recv.at[w],
                        device_id=(lax.rem(z + order[n], n_z) * n_y + y, sec),
                        device_id_type=MESH,
                    ).start()
        wait_bytes(recvz.at[w], z_recv.at[w])
        for n in range(n_z - 1):
            totals = [totals[m] + recvz[w, n, m].astype(F32) for m in range(2)]
        total = jnp.concatenate(totals, axis=0)
        if recent is not None:
            total = total + recent

        current = jnp.concatenate([local[b][m] for m in range(2) for b in range(own)], axis=0)
        moved = current + STEP_WIDTH * total
        high = moved.astype(BF16)
        low = (moved - high.astype(F32)).astype(BF16)
        new = lax.dot_general(
            jnp.concatenate([high, high, low], axis=1),
            advance,
            (((1,), (1,)), ((), ())),
            preferred_element_type=F32,
        )
        past.append(new)
        split = new.reshape(2, own, slab, pair)
        green = [[split[m, b] for m in range(2)] for b in range(own)]
        if w + 1 < steps:
            put_energy(w + 1, green)
            send_energy(w + 1)
        else:
            for b in range(own):
                for m in range(2):
                    out_ref[b, :, m * pair : (m + 1) * pair] = green[b][m]

    wait_bytes(vbuf.at[0 : n_hist - 1], v_send)
    for w in range(steps):
        wait_bytes(ebuf.at[w, 0 : times - slab], a_send.at[w])
        wait_bytes(recvb.at[w, 0 : n_hist - 1], b_send.at[w])
        wait_bytes(recvy.at[w], y_send.at[w])
        wait_bytes(recvz.at[w], z_send.at[w])


def body(n_hist, n_second, n_y, history, row_now, coupling, step_inverse, start_step, history_time):
    slots, orbitals, slab = history.shape[:3]
    own = row_now.shape[0]
    pair = 2 * orbitals
    n_z = n_hist // n_y
    steps = step_inverse.shape[0]
    times = slab * n_second
    rows = own * 2 * slab
    order = sorted(range(n_z), key=lambda d: (-min(d, n_z - d), d))
    cuts = ((0, n_z // 2), (n_z // 2, n_z))
    dims = (n_hist, n_second, n_y, tuple(order), cuts, steps)
    part = rows * n_z // len(cuts)
    blocks = history.reshape(slots * orbitals * slab * 2, pair)
    vmem = pl.BlockSpec(memory_space=pltpu.VMEM)
    dma = pltpu.SemaphoreType.DMA
    return pl.pallas_call(
        functools.partial(kernel, dims),
        out_shape=jax.ShapeDtypeStruct(row_now.shape, F32),
        in_specs=[pl.BlockSpec(memory_space=pltpu.HBM)] * 6,
        out_specs=vmem,
        scratch_shapes=[
            pltpu.VMEM(row_now.shape, F32),
            pltpu.VMEM(coupling.shape, F32),
            pltpu.VMEM(step_inverse.shape, F32),
            pltpu.SMEM(start_step.shape, jnp.int32),
            pltpu.SMEM(history_time.shape, jnp.int32),
            pltpu.VMEM(blocks.shape, BF16),
            pltpu.VMEM(blocks.shape, F32),
            pltpu.VMEM((len(cuts), n_y, part, pair * slots), BF16),
            pltpu.VMEM((steps, times, own * pair), BF16),
            pltpu.VMEM((n_hist, 8, times), F32),
            pltpu.VMEM((n_hist * 8 + 16, times), BF16),
            pltpu.VMEM((steps, n_hist, 16, pair), BF16),
            pltpu.VMEM((steps, n_hist, 16, pair), BF16),
            pltpu.VMEM((steps, len(cuts), n_y - 1, part, pair), BF16),
            pltpu.VMEM((steps, len(cuts), n_y - 1, part, pair), BF16),
            pltpu.VMEM((len(cuts), part, pair), F32),
            pltpu.VMEM((len(cuts), part, pair), F32),
            pltpu.VMEM((steps, n_z - 1, 2, own * slab, pair), BF16),
            pltpu.VMEM((steps, n_z - 1, 2, own * slab, pair), BF16),
            dma((6,)),
            dma,
            dma,
            dma((steps,)),
            dma((steps,)),
            dma((steps,)),
            dma((steps,)),
            dma((steps,)),
            dma((steps, len(cuts), 2)),
            dma((steps,)),
            dma((steps,)),
        ],
        compiler_params=pltpu.CompilerParams(
            collective_id=0, has_side_effects=True, vmem_limit_bytes=63 * 1024 * 1024
        ),
    )(blocks, row_now, coupling, step_inverse, start_step, history_time)


def solution(mesh):
    placed = (
        P("hist", None, "second", None, None),
        P("hist", "second", None),
        P("hist", None),
        P(),
        P(),
        P("hist"),
    )
    return jax.shard_map(
        functools.partial(body, mesh.shape["hist"], mesh.shape["second"], CHIPS_Y),
        mesh=mesh,
        in_specs=placed,
        out_specs=P("hist", "second", None),
        check_vma=False,
    )
```

```python
import functools

import jax
import jax.numpy as jnp
from jax import lax
from jax.experimental import pallas as pl
from jax.experimental.pallas import tpu as pltpu
from jax.sharding import PartitionSpec as P

MESH = pl.DeviceIdType.MESH
HIGHEST = lax.Precision.HIGHEST
STEP_WIDTH = 0.05
CHIPS_Y = 4
F32 = jnp.float32
BF16 = jnp.bfloat16


def cubic_term(first_real, first_imag, other_real, other_imag):
    square_real = first_real * first_real - first_imag * first_imag
    square_imag = 2.0 * first_real * first_imag
    return (
        square_real * other_real + square_imag * other_imag,
        square_imag * other_real - square_real * other_imag,
    )


def turned(pair, half):
    return jnp.concatenate([-pair[:, half:], pair[:, :half]], axis=1)


def wait_bytes(ref, sem):
    pltpu.make_async_copy(ref, ref, sem).wait()


def kernel(
    dims,
    hist_hbm,
    row_hbm,
    coup_hbm,
    inv_hbm,
    start_hbm,
    time_hbm,
    out_ref,
    row_ref,
    coup_ref,
    inv_ref,
    start_ref,
    time_ref,
    stored,
    spread,
    h2,
    ebuf,
    vbuf,
    onehot,
    sendb,
    recvb,
    sendy,
    recvy,
    zown,
    summed,
    sendz,
    recvz,
    in_sem,
    v_send,
    v_recv,
    a_send,
    a_recv,
    b_send,
    b_recv,
    y_send,
    y_recv,
    z_send,
    z_recv,
):
    n_hist, n_second, n_y, order, cuts, steps = dims
    n_z = n_hist // n_y
    own, slab, width = row_ref.shape
    half = width // 4
    pair = 2 * half
    slots = time_ref.shape[0]
    times = ebuf.shape[1]
    rows = own * 2 * slab
    h = lax.axis_index("hist")
    sec = lax.axis_index("second")
    z = h // n_y
    y = lax.rem(h, n_y)

    n_x = n_second // 2
    across = sorted(((dx, dc) for dx in range(n_x) for dc in range(2) if dx or dc), key=lambda d: -min(d[0], n_x - d[0]))

    def second_peer(d):
        return lax.rem(sec // 2 + d[0], n_x) * 2 + lax.rem(lax.rem(sec, 2) + d[1], 2)

    far_first = sorted(((dz, dy) for dz in range(n_z) for dy in range(n_y) if dz or dy), key=lambda d: -min(d[0], n_z - d[0]) - min(d[1], n_y - d[1]))

    barrier = pltpu.get_barrier_semaphore()

    for dz, dy in far_first:
        to = lax.rem(z + dz, n_z) * n_y + lax.rem(y + dy, n_y)
        pl.semaphore_signal(barrier, 1, device_id=(to, sec), device_id_type=MESH)

    for d in across:
        pl.semaphore_signal(barrier, 1, device_id=(h, second_peer(d)), device_id_type=MESH)

    loads = [
        pltpu.make_async_copy(src, dst, in_sem.at[i])
        for i, (src, dst) in enumerate(
            (
                (start_hbm, start_ref),
                (time_hbm, time_ref),
                (coup_hbm, coup_ref),
                (row_hbm, row_ref),
                (hist_hbm, stored),
                (inv_hbm, inv_ref),
            )
        )
    ]
    for load in loads:
        load.start()
    for load in loads[:4]:
        load.wait()

    anchor = start_ref[0].astype(F32)
    row8 = lax.broadcasted_iota(jnp.int32, (8, times), 0)
    tile = jnp.full((8, times), -1.0, F32)
    for s in range(slots):
        held = time_ref[s].astype(F32)
        tile = jnp.where(lax.rem(row8, slots) == s, held, tile)
    vbuf[h] = tile

    weight_sq = coup_ref[...] * coup_ref[...]

    def put_energy(w, green):
        for b in range(own):
            less, more = green[b][0], green[b][1]
            lr, li, mr, mi = less[:, :half], less[:, half:], more[:, :half], more[:, half:]
            less_r, less_i = cubic_term(lr, li, mr, mi)
            more_r, more_i = cubic_term(mr, mi, lr, li)
            weight = weight_sq[b : b + 1, :]
            both = jnp.concatenate([weight * (more_r - less_r), weight * (more_i - less_i)], axis=1)
            ebuf[w, pl.ds(pl.multiple_of(sec * slab, slab), slab), b * pair : (b + 1) * pair] = both.astype(BF16)

    def send_energy(w):
        mine = ebuf.at[w, pl.ds(pl.multiple_of(sec * slab, slab), slab)]

        for d in across:
            pltpu.make_async_remote_copy(
                mine, mine, a_send.at[w], a_recv.at[w], device_id=(h, second_peer(d)), device_id_type=MESH
            ).start()

    part = 2 * slab * (n_z // len(cuts)) * own
    green = [[row_ref[b, :, m * pair : (m + 1) * pair] for m in range(2)] for b in range(own)]
    put_energy(0, green)

    wide = 2 * slab
    loads[4].wait()

    @pl.loop(0, half)
    def _(j):
        for s in range(slots):
            at = pl.multiple_of((j * slots + s) * wide, wide)
            spread[pl.ds(at, wide), :] = stored[pl.ds(pl.multiple_of((s * half + j) * wide, wide), wide), :].astype(F32)

    pl.semaphore_wait(barrier, n_second - 1 + n_hist - 1)

    for dz, dy in far_first:
        to = lax.rem(z + dz, n_z) * n_y + lax.rem(y + dy, n_y)
        pltpu.make_async_remote_copy(
            vbuf.at[h], vbuf.at[h], v_send, v_recv, device_id=(to, sec), device_id_type=MESH
        ).start()

    send_energy(0)

    index = lax.broadcasted_iota(jnp.int32, (pair, pair), 0)
    place = lax.rem(index // own, n_z)
    depth = jnp.zeros_like(index)
    for n in range(n_z):
        depth = jnp.where(place == n, lax.rem(z + order[n], n_z), depth)
    to_y = lax.rem(lax.rem(index // (own * n_z), n_y) + y, n_y)
    column = ((depth * n_y + to_y) * own + lax.rem(index, own)) * 2 + index // half
    turn = jnp.where(lax.broadcasted_iota(jnp.int32, (pair, pair), 1) == column, 1.0, 0.0).astype(BF16)
    depth_of = half * slots
    unit = (n_z // len(cuts)) * own

    @pl.loop(0, slab // 2)
    def _(u):
        for m in range(2):
            both = []
            for k in range(2):
                block = spread[pl.ds((2 * u + k) * 2 + m, depth_of, stride=wide), :].astype(BF16)
                both.append(
                    lax.dot_general(turn, block, (((1,), (1,)), ((), ())), preferred_element_type=F32)
                )
            for p in range(2):
                for off in range(n_y):
                    for c in range(len(cuts)):
                        at = p * half + (off * len(cuts) + c) * unit
                        h2[
                            c,
                            off,
                            pl.ds(pl.multiple_of((m * slab + 2 * u) * unit, 2 * unit), 2 * unit),
                            p * depth_of : (p + 1) * depth_of,
                        ] = jnp.concatenate([one[at : at + unit] for one in both], axis=0).astype(BF16)

    wait_bytes(vbuf.at[0 : n_hist - 1], v_recv)
    asked = vbuf[...].reshape(n_hist * 8, times)
    lane = lax.broadcasted_iota(jnp.int32, (n_hist * 8, times), 1).astype(F32)
    onehot[0 : n_hist * 8, :] = jnp.where((asked == lane) & (asked <= anchor), 1.0, 0.0).astype(BF16)
    row16 = lax.broadcasted_iota(jnp.int32, (16, times), 0)
    lane16 = lax.broadcasted_iota(jnp.int32, (16, times), 1).astype(F32)
    later = anchor + 1.0 + lax.rem(row16, 2).astype(F32)
    onehot[n_hist * 8 : n_hist * 8 + 16, :] = jnp.where((later == lane16) & (row16 < 2 * own), 1.0, 0.0).astype(BF16)

    loads[5].wait()
    past = []
    for w in range(steps):
        wait_bytes(ebuf.at[w, 0 : times - slab], a_recv.at[w])
        picked = jnp.dot(onehot[...], ebuf[w], preferred_element_type=F32)
        sub = lax.rem(lax.broadcasted_iota(jnp.int32, (n_hist * 8, pair), 0), 8)
        chosen = jnp.where(sub < slots, picked[: n_hist * 8, :pair], picked[: n_hist * 8, pair:])
        sub8 = lax.broadcasted_iota(jnp.int32, (8, pair), 0)
        extra = picked[n_hist * 8 : n_hist * 8 + 8]
        extra = jnp.where(sub8 < 2, extra[:, :pair], extra[:, pair:])
        piece = jnp.concatenate(
            [chosen.reshape(n_hist, 8, pair), jnp.broadcast_to(extra[None], (n_hist, 8, pair))], axis=1
        )
        sendb[w] = piece.astype(BF16)

        for dz, dy in far_first:
            to = lax.rem(z + dz, n_z) * n_y + lax.rem(y + dy, n_y)
            pltpu.make_async_remote_copy(
                sendb.at[w, to], recvb.at[w, h], b_send.at[w], b_recv.at[w], device_id=(to, sec), device_id_type=MESH
            ).start()

        recvb[w, h] = sendb[w, h]
        wait_bytes(recvb.at[w, 0 : n_hist - 1], b_recv.at[w])
        got = recvb[w].astype(F32)
        left = got[:, :8].reshape(n_hist * 8, pair)
        weights = jnp.concatenate([left, turned(left, half)], axis=0).astype(BF16)

        for c in range(len(cuts)):
            def send(off, m, c=c):
                own_m = (w, c, off - 1, pl.ds(m * part // 2, part // 2))
                pltpu.make_async_remote_copy(
                    sendy.at[own_m],
                    recvy.at[own_m],
                    y_send.at[w],
                    y_recv.at[w, c, m],
                    device_id=(z * n_y + lax.rem(y + off, n_y), sec),
                    device_id_type=MESH,
                ).start()

            offs = sorted(range(1, n_y), key=lambda o: -min(o, n_y - o))
            for off in offs:
                sendy[w, c, off - 1] = jnp.dot(h2[c, off], weights, preferred_element_type=F32).astype(BF16)
                send(off, 0)
            for off in offs:
                send(off, 1)
        for c in range(len(cuts)):
            zown[c] = jnp.dot(h2[c, 0], weights, preferred_element_type=F32)

        local = [[green[b][m] for m in range(2)] for b in range(own)]
        recent = None
        if w:
            tail = got[:, 8:].reshape(n_hist * 8, pair).astype(BF16)
            rec = [None] * w
            for i in range(w):
                orbital = lax.broadcasted_iota(jnp.int32, (half, n_hist * 8), 0)
                at = lax.broadcasted_iota(jnp.int32, (half, n_hist * 8), 1)
                pick = jnp.where(at == (orbital // own) * 8 + lax.rem(orbital, own) * 2 + i, 1.0, 0.0).astype(BF16)
                column = jnp.dot(pick, tail, preferred_element_type=F32)
                matrix = jnp.concatenate([column, turned(column, half)], axis=0)
                rec[i] = jnp.dot(past[i], matrix, precision=HIGHEST, preferred_element_type=F32)
            recent = rec[0] if w == 1 else rec[0] + rec[1]

        real, imag = inv_ref[w, 0], inv_ref[w, 1]
        advance = jnp.concatenate(
            [jnp.concatenate([real, -imag], axis=1), jnp.concatenate([imag, real], axis=1)], axis=0
        )
        coarse = advance.astype(BF16)
        advance = jnp.concatenate([coarse, (advance - coarse.astype(F32)).astype(BF16), coarse], axis=1)
        totals = [None, None]
        for c, (first, last) in enumerate(cuts):
            for m in range(2):
                of_m = pl.ds(m * part // 2, part // 2)
                wait_bytes(recvy.at[w, c, :, of_m], y_recv.at[w, c, m])
                acc = zown[c, of_m]
                for k in range(n_y - 1):
                    acc = acc + recvy[w, c, k, of_m].astype(F32)
                summed[c, of_m] = acc
                for n in range(first, last):
                    piece = jnp.concatenate(
                        [
                            summed[c, pl.ds(m * part // 2 + (n - first) * own + b, slab, stride=unit), :]
                            for b in range(own)
                        ],
                        axis=0,
                    )
                    if order[n] == 0:
                        totals[m] = piece
                        continue
                    sendz[w, n, m] = piece.astype(BF16)
                    pltpu.make_async_remote_copy(
                        sendz.at[w, n, m],
                        recvz.at[w, n, m],
                        z_send.at[w],
                        z_recv.at[w],
                        device_id=(lax.rem(z + order[n], n_z) * n_y + y, sec),
                        device_id_type=MESH,
                    ).start()
        wait_bytes(recvz.at[w], z_recv.at[w])
        for n in range(n_z - 1):
            totals = [totals[m] + recvz[w, n, m].astype(F32) for m in range(2)]
        total = jnp.concatenate(totals, axis=0)
        if recent is not None:
            total = total + recent

        current = jnp.concatenate([local[b][m] for m in range(2) for b in range(own)], axis=0)
        moved = current + STEP_WIDTH * total
        high = moved.astype(BF16)
        low = (moved - high.astype(F32)).astype(BF16)
        new = lax.dot_general(
            jnp.concatenate([high, high, low], axis=1),
            advance,
            (((1,), (1,)), ((), ())),
            preferred_element_type=F32,
        )
        past.append(new)
        split = new.reshape(2, own, slab, pair)
        green = [[split[m, b] for m in range(2)] for b in range(own)]
        if w + 1 < steps:
            put_energy(w + 1, green)
            send_energy(w + 1)
        else:
            for b in range(own):
                for m in range(2):
                    out_ref[b, :, m * pair : (m + 1) * pair] = green[b][m]

    wait_bytes(vbuf.at[0 : n_hist - 1], v_send)
    for w in range(steps):
        wait_bytes(ebuf.at[w, 0 : times - slab], a_send.at[w])
        wait_bytes(recvb.at[w, 0 : n_hist - 1], b_send.at[w])
        wait_bytes(recvy.at[w], y_send.at[w])
        wait_bytes(recvz.at[w], z_send.at[w])


def body(n_hist, n_second, n_y, history, row_now, coupling, step_inverse, start_step, history_time):
    slots, orbitals, slab = history.shape[:3]
    own = row_now.shape[0]
    pair = 2 * orbitals
    n_z = n_hist // n_y
    steps = step_inverse.shape[0]
    times = slab * n_second
    rows = own * 2 * slab
    order = sorted(range(n_z), key=lambda d: (-min(d, n_z - d), d))
    cuts = ((0, n_z // 2), (n_z // 2, n_z))
    dims = (n_hist, n_second, n_y, tuple(order), cuts, steps)
    part = rows * n_z // len(cuts)
    blocks = history.reshape(slots * orbitals * slab * 2, pair)
    vmem = pl.BlockSpec(memory_space=pltpu.VMEM)
    dma = pltpu.SemaphoreType.DMA
    return pl.pallas_call(
        functools.partial(kernel, dims),
        out_shape=jax.ShapeDtypeStruct(row_now.shape, F32),
        in_specs=[pl.BlockSpec(memory_space=pltpu.HBM)] * 6,
        out_specs=vmem,
        scratch_shapes=[
            pltpu.VMEM(row_now.shape, F32),
            pltpu.VMEM(coupling.shape, F32),
            pltpu.VMEM(step_inverse.shape, F32),
            pltpu.SMEM(start_step.shape, jnp.int32),
            pltpu.SMEM(history_time.shape, jnp.int32),
            pltpu.VMEM(blocks.shape, BF16),
            pltpu.VMEM(blocks.shape, F32),
            pltpu.VMEM((len(cuts), n_y, part, pair * slots), BF16),
            pltpu.VMEM((steps, times, own * pair), BF16),
            pltpu.VMEM((n_hist, 8, times), F32),
            pltpu.VMEM((n_hist * 8 + 16, times), BF16),
            pltpu.VMEM((steps, n_hist, 16, pair), BF16),
            pltpu.VMEM((steps, n_hist, 16, pair), BF16),
            pltpu.VMEM((steps, len(cuts), n_y - 1, part, pair), BF16),
            pltpu.VMEM((steps, len(cuts), n_y - 1, part, pair), BF16),
            pltpu.VMEM((len(cuts), part, pair), F32),
            pltpu.VMEM((len(cuts), part, pair), F32),
            pltpu.VMEM((steps, n_z - 1, 2, own * slab, pair), BF16),
            pltpu.VMEM((steps, n_z - 1, 2, own * slab, pair), BF16),
            dma((6,)),
            dma,
            dma,
            dma((steps,)),
            dma((steps,)),
            dma((steps,)),
            dma((steps,)),
            dma((steps,)),
            dma((steps, len(cuts), 2)),
            dma((steps,)),
            dma((steps,)),
        ],
        compiler_params=pltpu.CompilerParams(
            collective_id=0, has_side_effects=True, vmem_limit_bytes=63 * 1024 * 1024
        ),
    )(blocks, row_now, coupling, step_inverse, start_step, history_time)


def solution(mesh):
    placed = (
        P("hist", None, "second", None, None),
        P("hist", "second", None),
        P("hist", None),
        P(),
        P(),
        P("hist"),
    )
    return jax.shard_map(
        functools.partial(body, mesh.shape["hist"], mesh.shape["second"], CHIPS_Y),
        mesh=mesh,
        in_specs=placed,
        out_specs=P("hist", "second", None),
        check_vma=False,
    )
```
